32 devices in a mesh: row: 4 (over y, x), col: 8 (over z, core).
Axes of the slice: x: 2, y: 2, z: 4, core: 2. Of those that a mesh axis runs over, the one named last changes fastest.
Arguments:
- chol: bfloat16 [6000, 8192], P('row', 'col'), may hold values from -1.75 to 1.75
- amplitudes: bfloat16 [8192, 4096], P('col', 'row'), may hold values from -0.0625 to 0.0625
- pair_offsets: int32 [4], replicated, may hold values from 0 to 8064
Outputs:
- residual: float32 [512, 4096], P('col', 'row')
The draws below stay inside these ranges and needn't reach their ends.
All inputs are finite; a program needn't handle non-finite values.
Results may differ from the reference program's by a relative error of at most 0.003.
Values may be sent and summed in bfloat16 or wider, within the bound.
No kernel may reach another device: no remote copies, remote signals or barrier semaphores. Data moves between devices by JAX's collectives and lax.ppermute only.
A program may use at most 64 MiB of HBM per device.

```python
import jax
import jax.numpy as jnp

NAUX = 6000
AB_TILE = 128
BLOCKS = 4
CD = 8192
IJ = 4096


def set_ends(drawn, rng, smallest, high):
    longest = drawn.shape.index(max(drawn.shape))
    spots = []
    for shift in (0, 1):
        where = [jax.random.randint(jax.random.fold_in(rng, axis), (), 0, length) for axis, length in enumerate(drawn.shape)]
        where[longest] = (where[longest] + shift) % drawn.shape[longest]
        spots.append(tuple(where))
    return drawn.at[spots[0]].set(smallest).at[spots[1]].set(high)


def level_of(rng, dims, split, low, top_value):
    def one(position, parts):
        steps = jax.random.uniform(jax.random.fold_in(jax.random.fold_in(rng, 6), position), (parts,), jnp.float32, low / len(split), top_value / len(split))
        return jnp.repeat(jnp.exp(steps), dims[position] // parts).reshape((-1,) + (1,) * (len(dims) - position - 1))

    factor_of = one(*split[0])
    for cut in split[1:]:
        factor_of = factor_of * one(*cut)
    return factor_of


def gaussian(own_key, shape, scale, bound, split=(), held_as=jnp.bfloat16):
    values = jax.random.normal(own_key, shape, jnp.float32) * scale
    if len(split) > 0:
        values = level_of(own_key, shape, split, -0.22, 0.18) * values
    return jnp.clip(values, min=-bound, max=bound).astype(held_as)


def setup_inputs(seed: int = 0) -> dict:
    keys = jax.random.split(jax.random.key(seed), 4)
    return {
        "chol": gaussian(keys[0], (NAUX, CD), (NAUX ** -0.25), 1.75, ((0, 4), (1, 8))),
        "amplitudes": gaussian(keys[1], (CD, IJ), CD ** -0.5, 0.0625, ((0, 8), (1, 4))),
        "pair_offsets": set_ends(jax.random.randint(keys[2], (BLOCKS,), 0, CD - AB_TILE + 1), jax.random.fold_in(keys[2], 1), 0, CD - AB_TILE).astype(jnp.int32),
    }


def reference(chol, amplitudes, pair_offsets):
    offsets = jnp.arange(AB_TILE, dtype=jnp.int32)
    rows = (pair_offsets.astype(jnp.int32)[:, None] + offsets[None, :]).reshape(-1)
    factors = jnp.take(chol, rows, axis=1)
    integrals = jnp.dot(factors.T, chol, preferred_element_type=jnp.float32).astype(jnp.bfloat16)
    return jnp.dot(integrals, amplitudes, preferred_element_type=jnp.float32)
```

```python
import jax
import jax.numpy as jnp
from jax import lax
from jax.sharding import PartitionSpec as P

AB_TILE = 128
CHUNKS = 2


def pairs(rows, cols, target):
    listed = []
    for row in range(rows):
        for col in range(cols):
            to = target(row, col // 2, col % 2)
            if to is not None:
                listed.append((row * cols + col, to[0] * cols + to[1] * 2 + to[2]))
    return listed


def pick(scalars, index):
    value = scalars[0]
    for place in range(1, len(scalars)):
        value = jnp.where(index == place, scalars[place], value)
    return value


def total(terms):
    value = terms[0]
    for term in terms[1:]:
        value = value + term
    return value


def flow(owners, places):
    upto = [total([(o <= p).astype(jnp.int32) for o in owners]) for p in range(places)]
    first = [jnp.int32(0)]
    for p in range(1, places):
        first.append(jnp.maximum(0, first[-1] + 1 - (upto[p] - upto[p - 1])))
    return upto, first


def make(rows, cols):
    places = cols // 2
    bits = rows.bit_length() - 1
    swap_core = pairs(rows, cols, lambda r, z, k: (r, z, 1 - k))
    along = pairs(
        rows, cols, lambda r, z, k: (r, z + 1 - 2 * k, k) if 0 <= z + 1 - 2 * k < places else None
    )
    in_plane = [
        pairs(rows, cols, lambda r, z, k, j=j: (r ^ (1 << (j if k == 0 else bits - 1 - j)), z, k))
        for j in range(bits)
    ]
    shifts = [
        pairs(rows, cols, lambda r, z, k, s=s: (r, (z + s) % places, k)) for s in range(places)
    ]
    axes = ("row", "col")

    def on_device(chol, amplitudes, pair_offsets):
        depth, width = chol.shape
        blocks = pair_offsets.shape[0]
        share = blocks * AB_TILE // cols
        part = share // CHUNKS
        unit = AB_TILE // CHUNKS
        row, col = lax.axis_index("row"), lax.axis_index("col")
        z, core = col // 2, col % 2

        offsets = [pair_offsets[b] for b in range(blocks)]
        ahead = [
            total(
                [
                    (offsets[c] < offsets[b] if c > b else offsets[c] <= offsets[b]).astype(jnp.int32)
                    for c in range(blocks)
                    if c != b
                ]
            )
            for b in range(blocks)
        ]
        chip = 2 * width
        up = flow([o // chip for o in offsets], places)
        down = flow([places - 1 - (o + AB_TILE - 1) // chip for o in offsets], places)
        position = jnp.where(core == 0, z, places - 1 - z)
        upto = [jnp.where(core == 0, a, b) for a, b in zip(up[0], down[0])]
        first = [jnp.where(core == 0, a, b) for a, b in zip(up[1], down[1])]
        rank = [jnp.where(core == 0, blocks - 1 - a, a) for a in ahead]
        need = jnp.int32(0)
        for counts, starts in (up, down):
            for p in range(places - 1):
                need = jnp.maximum(need, counts[p] + starts[p])

        def sent(p, slot):
            q = blocks - pick(upto, p) + slot - pick(first, p)
            good = (slot >= pick(first, p)) & (q < blocks) & (p >= 0)
            b = total([jnp.where(rank[b] == q, b, 0) for b in range(blocks)])
            return jnp.where(good, b, blocks)

        local = col * width + lax.broadcasted_iota(jnp.int32, (1, width), 1)
        own = []
        for h in range(CHUNKS):
            place = jnp.arange(AB_TILE, dtype=jnp.int32).reshape(-1, CHUNKS, part)[:, h].reshape(-1)
            wanted = (pair_offsets[:, None] + place[None, :]).reshape(-1, 1)
            selector = (local == wanted).astype(jnp.bfloat16)
            own.append(
                lax.dot_general(
                    selector, chol, (((1,), (1,)), ((), ())), preferred_element_type=jnp.float32
                ).astype(jnp.bfloat16)
            )
        own = [o + lax.ppermute(o, axes, swap_core) for o in own]
        own = [o.reshape(blocks, unit, depth) for o in own]

        def rest(slots):
            came = [jnp.zeros((blocks + 1, unit, depth), jnp.bfloat16) for _ in range(CHUNKS)]
            for slot in range(slots):
                b = jnp.minimum(sent(position, slot), blocks - 1)
                r = sent(position - 1, slot)
                for h in range(CHUNKS):
                    payload = lax.dynamic_index_in_dim(own[h], b, 0, False)
                    if slot > 0:
                        payload = payload + lax.dynamic_index_in_dim(came[h], b, 0, False)
                    got = lax.ppermute(payload, axes, along)
                    came[h] = lax.dynamic_update_index_in_dim(came[h], got, r, 0)
            done = []
            for h in range(CHUNKS):
                mine = came[h][:blocks]
                factors = own[h] + mine + lax.ppermute(mine, axes, swap_core)
                factors = factors.reshape(blocks * unit, depth)
                block = jnp.dot(factors, chol, preferred_element_type=jnp.float32)
                turns = []
                for j in range(bits):
                    bit = jnp.where(core == 0, j, bits - 1 - j)
                    turn = (row >> bit) & 1
                    turns.append(turn)
                    halves = block.reshape(2, -1, width)
                    give = lax.dynamic_index_in_dim(halves, 1 - turn, 0, False)
                    keep = lax.dynamic_index_in_dim(halves, turn, 0, False)
                    block = keep + lax.ppermute(give, axes, in_plane[j])
                block = block.astype(jnp.bfloat16)
                for j in reversed(range(bits)):
                    got = lax.ppermute(block, axes, in_plane[j])
                    low = jnp.where(turns[j] == 0, block, got)
                    high = jnp.where(turns[j] == 0, got, block)
                    block = jnp.concatenate([low, high], 0)
                result = jnp.dot(block, amplitudes, preferred_element_type=jnp.float32)
                result = result.reshape(places, 2, part, -1)
                give = lax.dynamic_index_in_dim(result, 1 - core, 1, False)
                keep = lax.dynamic_index_in_dim(result, core, 1, False)
                result = keep + lax.ppermute(give, axes, swap_core)
                sums = lax.dynamic_index_in_dim(result, z, 0, False)
                for s in range(1, places):
                    to = lax.rem(z + s, places)
                    give = lax.dynamic_index_in_dim(result, to, 0, False).astype(jnp.bfloat16)
                    sums = sums + lax.ppermute(give, axes, shifts[s]).astype(jnp.float32)
                done.append(sums)
            return jnp.concatenate(done, 0)

        most = blocks + places - 2
        short = min(blocks, most)
        return lax.cond(need <= short, lambda: rest(short), lambda: rest(most))

    return on_device


def solution(mesh):
    placed = (P("row", "col"), P("col", "row"), P())
    body = make(mesh.shape["row"], mesh.shape["col"])
    return jax.shard_map(
        body, mesh=mesh, in_specs=placed, out_specs=P("col", "row"), check_vma=False
    )
```

```python
import functools

import jax
import jax.numpy as jnp
from jax import lax
from jax.experimental import pallas as pl
from jax.experimental.pallas import tpu as pltpu
from jax.sharding import PartitionSpec as P

AB_TILE = 128
CHUNKS = 2
AXES = ("row", "col")
VMEM = pltpu.CompilerParams(vmem_limit_bytes=20 * 1024 * 1024)


def pairs(rows, cols, target):
    listed = []
    for row in range(rows):
        for col in range(cols):
            to = target(row, col // 2, col % 2)
            listed.append((row * cols + col, to[0] * cols + to[1] * 2 + to[2]))
    return listed


def entry(offsets, chip, width, index):
    low = chip * (2 * width)
    seen = jnp.int32(0)
    block = jnp.int32(0)
    for b in range(offsets.shape[0]):
        start = offsets[b]
        here = ((start < low + 2 * width) & (start + (AB_TILE - 1) >= low)).astype(jnp.int32)
        block = jnp.where((here == 1) & (seen == index), b, block)
        seen = seen + here
    return block, seen > index


def pick_kernel(chunk, share, offsets, chol, keep, give):
    cap, unit, depth = keep.shape
    width = chol.shape[1]
    part = share // CHUNKS
    col = lax.axis_index("col")
    chip, core = lax.div(col, 2), lax.rem(col, 2)
    window = 2 * AB_TILE
    t = lax.broadcasted_iota(jnp.int32, (unit, window), 0)
    lane = lax.broadcasted_iota(jnp.int32, (unit, window), 1)
    place = lax.div(t, part) * share + chunk * part + lax.rem(t, part)
    for slot in range(cap):
        for ref, parity in ((give, 1 - core), (keep, core)):
            block, there = entry(offsets, chip, width, 2 * slot + parity)
            start = offsets[block] - col * width
            left = jnp.clip(lax.shift_right_arithmetic(start, 7), 0, width // AB_TILE - 2)
            left = pl.multiple_of(left * AB_TILE, AB_TILE)
            start = jnp.where(there, start, -4 * AB_TILE - width)
            hit = (lane + left == place + start).astype(jnp.float32).astype(jnp.bfloat16)
            ref[slot] = lax.dot_general(
                hit,
                chol[:, pl.ds(left, window)],
                (((1,), (1,)), ((), ())),
                preferred_element_type=jnp.float32,
            ).astype(jnp.bfloat16)


def integrals_kernel(places, offsets, *refs):
    mine, other = refs[:places], refs[places : 2 * places]
    chol, block_out, factors = refs[2 * places :]
    cap, unit, depth = mine[0].shape
    width = chol.shape[1]
    col = lax.axis_index("col")
    chip, core = lax.div(col, 2), lax.rem(col, 2)
    factors[...] = jnp.zeros_like(factors)
    for j in range(places):
        for group, parity in ((mine, core), (other, 1 - core)):
            for slot in range(cap):
                block, there = entry(offsets, lax.bitwise_xor(chip, j), width, 2 * slot + parity)

                @pl.when(there)
                def _():
                    at = pl.ds(pl.multiple_of(block * unit, unit), unit)
                    factors[at, :] += group[j][slot]

    block_out[...] = jnp.dot(factors[...], chol[...], preferred_element_type=jnp.float32)


def residual_kernel(block, amplitudes, keep, give, result):
    core = lax.rem(lax.axis_index("col"), 2)
    places, part, _ = keep.shape
    result[...] = jnp.dot(block[...], amplitudes[...], preferred_element_type=jnp.float32)
    for p in range(places):
        keep[p] = result[pl.ds(pl.multiple_of(p * 2 * part + core * part, part), part), :]
        give[p] = result[pl.ds(pl.multiple_of(p * 2 * part + (1 - core) * part, part), part), :]


def split_kernel(keep, came, own, *gives):
    chip = lax.div(lax.axis_index("col"), 2)
    own[...] = keep[chip] + came[chip]
    for j, give in enumerate(gives, 1):
        to = lax.bitwise_xor(chip, j)
        give[...] = (keep[to] + came[to]).astype(jnp.bfloat16)


def final_kernel(terms, *refs):
    out = refs[-1]
    part = refs[0].shape[0]
    for h in range(CHUNKS):
        group = refs[h * terms : (h + 1) * terms]
        value = group[0][...]
        for ref in group[1:]:
            value = value + ref[...].astype(jnp.float32)
        out[h * part : (h + 1) * part, :] = value


def call(kernel, outs, smem, *args, scratch=(), flops=0):
    size = sum(a.size * a.dtype.itemsize for a in args)
    return pl.pallas_call(
        kernel,
        out_shape=outs,
        in_specs=[pl.BlockSpec(memory_space=pltpu.SMEM)] * smem
        + [pl.BlockSpec(memory_space=pltpu.VMEM)] * (len(args) - smem),
        scratch_shapes=list(scratch),
        compiler_params=VMEM,
        cost_estimate=pl.CostEstimate(flops=flops, bytes_accessed=size, transcendentals=0),
    )(*args)


def scaled(value, top):
    power = jnp.clip(jnp.floor(14.0 - jnp.log2(jnp.maximum(top, 1e-30))), -100.0, 100.0)
    body = (value * jnp.exp2(power)).astype(jnp.float16)
    return jnp.concatenate([body, jnp.full((16, value.shape[1]), power, jnp.float16)], 0)


def unscaled(sent):
    power = sent[-1, 0].astype(jnp.float32)
    return sent[:-16].astype(jnp.float32) * jnp.exp2(-power), power


def make(rows, cols):
    places = cols // 2
    bits = rows.bit_length() - 1
    swap_core = pairs(rows, cols, lambda r, z, k: (r, z, 1 - k))
    in_plane = [
        pairs(rows, cols, lambda r, z, k, j=j: (r ^ (1 << (j if k == 0 else bits - 1 - j)), z, k))
        for j in range(bits)
    ]
    jumps = [pairs(rows, cols, lambda r, z, k, j=j: (r, z ^ j, k)) for j in range(places)]

    def on_device(chol, amplitudes, pair_offsets):
        depth, width = chol.shape
        columns = amplitudes.shape[1]
        blocks = pair_offsets.shape[0]
        share = blocks * AB_TILE // cols
        part = share // CHUNKS
        unit = AB_TILE // CHUNKS
        height = blocks * unit

        def rest(cap):
            held = jax.ShapeDtypeStruct((cap, unit, depth), jnp.bfloat16)
            done = []
            for h in range(CHUNKS):
                keep, give = call(
                    functools.partial(pick_kernel, h, share), (held, held), 1, pair_offsets, chol
                )
                own = keep + lax.ppermute(give, AXES, swap_core)
                mine = [own] + [lax.ppermute(own, AXES, jumps[j]) for j in range(1, places)]
                other = [lax.ppermute(m, AXES, swap_core) for m in mine]
                block = call(
                    functools.partial(integrals_kernel, places),
                    jax.ShapeDtypeStruct((height, width), jnp.float32),
                    1,
                    pair_offsets,
                    *mine,
                    *other,
                    chol,
                    scratch=[pltpu.VMEM((height, depth), jnp.bfloat16)],
                    flops=2 * height * depth * width,
                )
                top = jnp.max(jnp.abs(block))
                for j in range(bits):
                    came, power = unscaled(lax.ppermute(scaled(block, top), AXES, in_plane[j]))
                    block = block + came
                    top = top + jnp.exp2(15.0 - power)
                keep, give = call(
                    residual_kernel,
                    (jax.ShapeDtypeStruct((places, part, columns), jnp.float32),) * 2,
                    0,
                    block.astype(jnp.bfloat16),
                    amplitudes,
                    scratch=[pltpu.VMEM((height, columns), jnp.float32)],
                    flops=2 * height * width * columns,
                )
                came = lax.ppermute(give, AXES, swap_core)
                sums, *gives = call(
                    split_kernel,
                    (jax.ShapeDtypeStruct((part, columns), jnp.float32),)
                    + (jax.ShapeDtypeStruct((part, columns), jnp.bfloat16),) * (places - 1),
                    0,
                    keep,
                    came,
                )
                done += [sums] + [lax.ppermute(g, AXES, jumps[j]) for j, g in enumerate(gives, 1)]
            return call(
                functools.partial(final_kernel, places),
                jax.ShapeDtypeStruct((share, columns), jnp.float32),
                0,
                *done,
            )

        chips = jnp.arange(places, dtype=jnp.int32)[:, None] * (2 * width)
        starts = pair_offsets[None, :]
        touch = (starts < chips + 2 * width) & (starts + (AB_TILE - 1) >= chips)
        most = jnp.max(jnp.sum(touch.astype(jnp.int32), 1))
        return lax.cond(most <= 2, lambda: rest(1), lambda: rest((blocks + 1) // 2))

    return on_device


def simple(chol, amplitudes, pair_offsets):
    width = chol.shape[1]
    rows = (pair_offsets[:, None] + jnp.arange(AB_TILE, dtype=jnp.int32)[None, :]).reshape(-1)
    local = lax.axis_index("col") * width + jnp.arange(width, dtype=jnp.int32)
    selector = (local[:, None] == rows[None, :]).astype(jnp.bfloat16)
    picked = jnp.dot(chol, selector, preferred_element_type=jnp.float32)
    factors = lax.psum(picked.astype(jnp.bfloat16), "col")
    block = jnp.dot(factors.T, chol, preferred_element_type=jnp.float32)
    block = lax.psum(block, "row").astype(jnp.bfloat16)
    return lax.psum_scatter(
        jnp.dot(block, amplitudes, preferred_element_type=jnp.float32),
        "col",
        scatter_dimension=0,
        tiled=True,
    )


def solution(mesh):
    rows, cols = mesh.shape["row"], mesh.shape["col"]
    body = make(rows, cols) if (rows, cols) == (4, 8) else simple
    return jax.shard_map(
        body,
        mesh=mesh,
        in_specs=(P("row", "col"), P("col", "row"), P()),
        out_specs=P("col", "row"),
        check_vma=False,
    )
```

```python
import functools

import jax
import jax.numpy as jnp
from jax import lax
from jax.experimental import pallas as pl
from jax.experimental.pallas import tpu as pltpu
from jax.sharding import PartitionSpec as P

AB_TILE = 128
SPLIT = (5, 3)
PAD = 16
AXES = ("row", "col")
VMEM = pltpu.CompilerParams(vmem_limit_bytes=20 * 1024 * 1024)


def pairs(rows, cols, target):
    listed = []
    for row in range(rows):
        for col in range(cols):
            to = target(row, col // 2, col % 2)
            listed.append((row * cols + col, to[0] * cols + to[1] * 2 + to[2]))
    return listed


def entry(offsets, chip, width, index):
    low = chip * (2 * width)
    seen = jnp.int32(0)
    block = jnp.int32(0)
    for b in range(offsets.shape[0]):
        start = offsets[b]
        here = ((start < low + 2 * width) & (start + (AB_TILE - 1) >= low)).astype(jnp.int32)
        block = jnp.where((here == 1) & (seen == index), b, block)
        seen = seen + here
    return block, seen > index


def pick_kernel(base, part, share, offsets, chol, keep, give, *most):
    cap, unit, depth = keep.shape
    width = chol.shape[1]
    col = lax.axis_index("col")
    chip, core = lax.div(col, 2), lax.rem(col, 2)
    window = 2 * AB_TILE
    t = lax.broadcasted_iota(jnp.int32, (unit, window), 0)
    lane = lax.broadcasted_iota(jnp.int32, (unit, window), 1)
    place = lax.div(t, part) * share + base + lax.rem(t, part)
    for slot in range(cap):
        for ref, parity in ((give, 1 - core), (keep, core)):
            block, there = entry(offsets, chip, width, 2 * slot + parity)
            start = offsets[block] - col * width
            left = jnp.clip(lax.shift_right_arithmetic(start, 7), 0, width // AB_TILE - 2)
            left = pl.multiple_of(left * AB_TILE, AB_TILE)
            start = jnp.where(there, start, -4 * AB_TILE - width)
            hit = (lane + left == place + start).astype(jnp.float32).astype(jnp.bfloat16)
            ref[slot] = lax.dot_general(
                hit,
                chol[:, pl.ds(left, window)],
                (((1,), (1,)), ((), ())),
                preferred_element_type=jnp.float32,
            ).astype(jnp.bfloat16)
    for ref in most:
        value = jnp.int32(0)
        for place in range(lax.axis_size("col") // 2):
            low = place * 2 * width
            seen = jnp.int32(0)
            for b in range(offsets.shape[0]):
                here = (offsets[b] < low + 2 * width) & (offsets[b] + (AB_TILE - 1) >= low)
                seen = seen + here.astype(jnp.int32)
            value = jnp.maximum(value, seen)
        ref[0] = value


def integrals_kernel(places, offsets, *refs):
    mine, other = refs[:places], refs[places : 2 * places]
    chol, block_out, factors = refs[2 * places :]
    cap, unit, depth = mine[0].shape
    width = chol.shape[1]
    col = lax.axis_index("col")
    chip, core = lax.div(col, 2), lax.rem(col, 2)
    factors[...] = jnp.zeros_like(factors)
    for j in range(places):
        for group, parity in ((mine, core), (other, 1 - core)):
            for slot in range(cap):
                block, there = entry(offsets, lax.bitwise_xor(chip, j), width, 2 * slot + parity)

                @pl.when(there)
                def _():
                    at = pl.ds(pl.multiple_of(block * unit, unit), unit)
                    factors[at, :] += group[j][slot]

    height = factors.shape[0]
    value = jnp.dot(factors[...], chol[...], preferred_element_type=jnp.float32)
    top = jnp.max(jnp.max(jnp.abs(value), axis=0, keepdims=True), axis=1, keepdims=True)
    power = jnp.floor(14.0 - jnp.log2(jnp.maximum(top, 1e-30)))
    power = jnp.broadcast_to(jnp.clip(power, -100.0, 100.0), (1, width))
    block_out[:height, :] = value * jnp.exp2(power)
    block_out[height:, :] = jnp.broadcast_to(power, (PAD, width))


def join_kernel(own, came, total):
    height = own.shape[0] - PAD
    first, second = own[height : height + 1, :], came[height : height + 1, :]
    power = jnp.minimum(first, second) - 1.0
    total[:height, :] = own[:height, :] * jnp.exp2(power - first) + came[:height, :] * jnp.exp2(power - second)
    total[height:, :] = jnp.broadcast_to(power, (PAD, own.shape[1]))


def residual_kernel(own, came, amplitudes, keep, give, result):
    core = lax.rem(lax.axis_index("col"), 2)
    places, part, _ = keep.shape
    height = own.shape[0] - PAD
    first, second = own[height : height + 1, :], came[height : height + 1, :]
    block = own[:height, :] * jnp.exp2(-first) + came[:height, :] * jnp.exp2(-second)
    result[...] = jnp.dot(
        block.astype(jnp.bfloat16), amplitudes[...], preferred_element_type=jnp.float32
    )
    for p in range(places):
        keep[p] = result[pl.ds(pl.multiple_of(p * 2 * part + core * part, part), part), :]
        give[p] = result[pl.ds(pl.multiple_of(p * 2 * part + (1 - core) * part, part), part), :]


def split_kernel(keep, came, own, *gives):
    chip = lax.div(lax.axis_index("col"), 2)
    own[...] = keep[chip] + came[chip]
    for j, give in enumerate(gives, 1):
        to = lax.bitwise_xor(chip, j)
        give[...] = (keep[to] + came[to]).astype(jnp.bfloat16)


def final_kernel(terms, *refs):
    out = refs[-1]
    base = 0
    for h in range(len(SPLIT)):
        group = refs[h * terms : (h + 1) * terms]
        value = group[0][...]
        for ref in group[1:]:
            value = value + ref[...].astype(jnp.float32)
        out[base : base + value.shape[0], :] = value
        base += value.shape[0]


def call(kernel, outs, smem, *args, scratch=(), flops=0):
    size = sum(a.size * a.dtype.itemsize for a in args)
    place = lambda o: pl.BlockSpec(memory_space=pltpu.SMEM if o.dtype == jnp.int32 else pltpu.VMEM)
    return pl.pallas_call(
        kernel,
        out_shape=outs,
        out_specs=jax.tree.map(place, outs),
        in_specs=[pl.BlockSpec(memory_space=pltpu.SMEM)] * smem
        + [pl.BlockSpec(memory_space=pltpu.VMEM)] * (len(args) - smem),
        scratch_shapes=list(scratch),
        compiler_params=VMEM,
        cost_estimate=pl.CostEstimate(flops=flops, bytes_accessed=size, transcendentals=0),
    )(*args)


def make(rows, cols):
    places = cols // 2
    bits = 2
    swap_core = pairs(rows, cols, lambda r, z, k: (r, z, 1 - k))
    in_plane = [
        pairs(rows, cols, lambda r, z, k, j=j: (r ^ (1 << (j if k == 0 else bits - 1 - j)), z, k))
        for j in range(bits)
    ]
    jumps = [pairs(rows, cols, lambda r, z, k, j=j: (r, z ^ j, k)) for j in range(places)]

    def on_device(chol, amplitudes, pair_offsets):
        depth, width = chol.shape
        columns = amplitudes.shape[1]
        blocks = pair_offsets.shape[0]
        share = blocks * AB_TILE // cols
        parts = [share * eighths // 8 for eighths in SPLIT]

        def picked(cap, h, offsets, most=()):
            held = jax.ShapeDtypeStruct((cap, AB_TILE // share * parts[h], depth), jnp.bfloat16)
            kernel = functools.partial(pick_kernel, sum(parts[:h]), parts[h], share)
            keep, give, *most = call(kernel, (held, held, *most), 1, offsets, chol)
            return (keep + lax.ppermute(give, AXES, swap_core), *most)

        def rest(cap, own):
            def jump(own, j):
                return lax.ppermute(own, AXES, jumps[j])

            def integrals(mine):
                height = blocks * mine[0].shape[1]
                other = [lax.ppermute(m, AXES, swap_core) for m in mine]
                return call(
                    functools.partial(integrals_kernel, places),
                    jax.ShapeDtypeStruct((height + PAD, width), jnp.float32),
                    1,
                    pair_offsets,
                    *mine,
                    *other,
                    chol,
                    scratch=[pltpu.VMEM((height, depth), jnp.bfloat16)],
                    flops=2 * height * depth * width,
                )

            def swap(block, j):
                came = lax.ppermute(block.astype(jnp.float16), AXES, in_plane[j])
                return came.astype(jnp.float32)

            def join(block, came):
                return call(join_kernel, jax.ShapeDtypeStruct(block.shape, jnp.float32), 0, block, came)

            def residual(block, came, part):
                height = block.shape[0] - PAD
                return call(
                    residual_kernel,
                    (jax.ShapeDtypeStruct((places, part, columns), jnp.float32),) * 2,
                    0,
                    block,
                    came,
                    amplitudes,
                    scratch=[pltpu.VMEM((height, columns), jnp.float32)],
                    flops=2 * height * width * columns,
                )

            def split(keep, got):
                part = keep.shape[1]
                return call(
                    split_kernel,
                    (jax.ShapeDtypeStruct((part, columns), jnp.float32),)
                    + (jax.ShapeDtypeStruct((part, columns), jnp.bfloat16),) * (places - 1),
                    0,
                    keep,
                    got,
                )

            def deliver(gives):
                return [lax.ppermute(g, AXES, jumps[j]) for j, g in enumerate(gives, 1)]

            after = lax.optimization_barrier
            mine = [own] + [jump(own, j) for j in range(1, places)]
            offsets, _ = after((pair_offsets, mine[1]))
            (own,) = picked(cap, 1, offsets)
            own, *mine = after((own, *mine))
            block = integrals(mine)
            far = jump(own, places - 1)
            came = swap(block, 0)
            came, far = after((came, far))
            block = join(block, came)
            near, _ = after((own, block))
            near = [jump(near, j) for j in range(1, places - 1)]
            came = swap(block, 1)
            keep, give = residual(block, came, parts[0])
            got = lax.ppermute(give, AXES, swap_core)
            own, far, *near, _ = after((own, far, *near, give))
            second = integrals([own, *near, far])
            second, _ = after((second, came))
            came = swap(second, 0)
            sums, *gives = split(keep, got)
            done = [sums] + deliver(gives)
            second = join(second, came)
            second, *done = after((second, *done))
            came = swap(second, 1)
            keep, give = residual(second, came, parts[1])
            sums, *gives = split(keep, lax.ppermute(give, AXES, swap_core))
            done += [sums] + deliver(gives)
            return call(
                functools.partial(final_kernel, places),
                jax.ShapeDtypeStruct((share, columns), jnp.float32),
                0,
                *done,
            )

        own, most = picked(1, 0, pair_offsets, (jax.ShapeDtypeStruct((1,), jnp.int32),))
        return lax.cond(
            most[0] <= 2,
            lambda own: rest(1, own),
            lambda own: rest((blocks + 1) // 2, *picked((blocks + 1) // 2, 0, pair_offsets)),
            own,
        )

    return on_device


def simple(chol, amplitudes, pair_offsets):
    width = chol.shape[1]
    rows = (pair_offsets[:, None] + jnp.arange(AB_TILE, dtype=jnp.int32)[None, :]).reshape(-1)
    local = lax.axis_index("col") * width + jnp.arange(width, dtype=jnp.int32)
    selector = (local[:, None] == rows[None, :]).astype(jnp.bfloat16)
    picked = jnp.dot(chol, selector, preferred_element_type=jnp.float32)
    factors = lax.psum(picked.astype(jnp.bfloat16), "col")
    block = jnp.dot(factors.T, chol, preferred_element_type=jnp.float32)
    block = lax.psum(block, "row").astype(jnp.bfloat16)
    return lax.psum_scatter(
        jnp.dot(block, amplitudes, preferred_element_type=jnp.float32),
        "col",
        scatter_dimension=0,
        tiled=True,
    )


def solution(mesh):
    rows, cols = mesh.shape["row"], mesh.shape["col"]
    body = make(rows, cols) if (rows, cols) == (4, 8) else simple
    return jax.shard_map(
        body,
        mesh=mesh,
        in_specs=(P("row", "col"), P("col", "row"), P()),
        out_specs=P("col", "row"),
        check_vma=False,
    )
```

```python
import functools

import jax
import jax.numpy as jnp
from jax import lax
from jax.experimental import pallas as pl
from jax.experimental.pallas import tpu as pltpu
from jax.sharding import PartitionSpec as P

AB_TILE = 128
SPLIT = (5, 3)
PAD = 16
AXES = ("row", "col")
VMEM = pltpu.CompilerParams(vmem_limit_bytes=20 * 1024 * 1024)


def pairs(rows, cols, target):
    listed = []
    for row in range(rows):
        for col in range(cols):
            to = target(row, col // 2, col % 2)
            listed.append((row * cols + col, to[0] * cols + to[1] * 2 + to[2]))
    return listed


def entry(offsets, chip, width, index):
    low = chip * (2 * width)
    seen = jnp.int32(0)
    block = jnp.int32(0)
    for b in range(offsets.shape[0]):
        start = offsets[b]
        here = ((start < low + 2 * width) & (start + (AB_TILE - 1) >= low)).astype(jnp.int32)
        block = jnp.where((here == 1) & (seen == index), b, block)
        seen = seen + here
    return block, seen > index


def pick_kernel(base, part, share, offsets, chol, keep, give, *refs):
    *most, held, done = refs
    cap, unit, depth = keep.shape
    width = chol.shape[1]
    col = lax.axis_index("col")
    chip, core = lax.div(col, 2), lax.rem(col, 2)
    window = 2 * AB_TILE
    t = lax.broadcasted_iota(jnp.int32, (unit, window), 0)
    lane = lax.broadcasted_iota(jnp.int32, (unit, window), 1)
    place = lax.div(t, part) * share + base + lax.rem(t, part)
    jobs = []
    for slot in range(cap):
        for ref, parity in ((give, 1 - core), (keep, core)):
            block, there = entry(offsets, chip, width, 2 * slot + parity)
            start = offsets[block] - col * width
            left = jnp.clip(lax.shift_right_arithmetic(start, 7), 0, width // AB_TILE - 2)
            left = pl.multiple_of(left * AB_TILE, AB_TILE)
            start = jnp.where(there, start, -4 * AB_TILE - width)
            at = len(jobs)
            copy = pltpu.make_async_copy(chol.at[:, pl.ds(left, window)], held.at[at], done.at[at])
            copy.start()
            jobs.append((copy, ref, slot, start - left))
    for at, (copy, ref, slot, start) in enumerate(jobs):
        hit = (lane == place + start).astype(jnp.float32).astype(jnp.bfloat16)
        copy.wait()
        ref[slot] = lax.dot_general(
            hit, held[at], (((1,), (1,)), ((), ())), preferred_element_type=jnp.float32
        ).astype(jnp.bfloat16)
    for ref in most:
        value = jnp.int32(0)
        for place in range(lax.axis_size("col") // 2):
            low = place * 2 * width
            seen = jnp.int32(0)
            for b in range(offsets.shape[0]):
                here = (offsets[b] < low + 2 * width) & (offsets[b] + (AB_TILE - 1) >= low)
                seen = seen + here.astype(jnp.int32)
            value = jnp.maximum(value, seen)
        ref[0] = value


def integrals_kernel(places, offsets, *refs):
    mine, other = refs[:places], refs[places : 2 * places]
    chol, block_out, factors = refs[2 * places :]
    cap, unit, depth = mine[0].shape
    width = chol.shape[1]
    col = lax.axis_index("col")
    chip, core = lax.div(col, 2), lax.rem(col, 2)
    factors[...] = jnp.zeros_like(factors)
    for j in range(places):
        for group, parity in ((mine, core), (other, 1 - core)):
            for slot in range(cap):
                block, there = entry(offsets, lax.bitwise_xor(chip, j), width, 2 * slot + parity)

                @pl.when(there)
                def _():
                    at = pl.ds(pl.multiple_of(block * unit, unit), unit)
                    factors[at, :] += group[j][slot]

    height = factors.shape[0]
    value = jnp.dot(factors[...], chol[...], preferred_element_type=jnp.float32)
    top = jnp.max(jnp.max(jnp.abs(value), axis=0, keepdims=True), axis=1, keepdims=True)
    power = jnp.floor(14.0 - jnp.log2(jnp.maximum(top, 1e-30)))
    power = jnp.broadcast_to(jnp.clip(power, -100.0, 100.0), (1, width))
    block_out[:height, :] = value * jnp.exp2(power)
    block_out[height:, :] = jnp.broadcast_to(power, (PAD, width))


def join_kernel(own, came, total):
    height = own.shape[0] - PAD
    first, second = own[height : height + 1, :], came[height : height + 1, :]
    power = jnp.minimum(first, second) - 1.0
    total[:height, :] = own[:height, :] * jnp.exp2(power - first) + came[:height, :] * jnp.exp2(power - second)
    total[height:, :] = jnp.broadcast_to(power, (PAD, own.shape[1]))


def residual_kernel(own, came, amplitudes, keep, give, result):
    core = lax.rem(lax.axis_index("col"), 2)
    places, part, _ = keep.shape
    height = own.shape[0] - PAD
    first, second = own[height : height + 1, :], came[height : height + 1, :]
    block = own[:height, :] * jnp.exp2(-first) + came[:height, :] * jnp.exp2(-second)
    result[...] = jnp.dot(
        block.astype(jnp.bfloat16), amplitudes[...], preferred_element_type=jnp.float32
    )
    for p in range(places):
        keep[p] = result[pl.ds(pl.multiple_of(p * 2 * part + core * part, part), part), :]
        give[p] = result[pl.ds(pl.multiple_of(p * 2 * part + (1 - core) * part, part), part), :]


def split_kernel(keep, came, own, *gives):
    chip = lax.div(lax.axis_index("col"), 2)
    own[...] = keep[chip] + came[chip]
    for j, give in enumerate(gives, 1):
        to = lax.bitwise_xor(chip, j)
        give[...] = (keep[to] + came[to]).astype(jnp.bfloat16)


def final_kernel(terms, *refs):
    out = refs[-1]
    base = 0
    for h in range(len(SPLIT)):
        group = refs[h * terms : (h + 1) * terms]
        value = group[0][...]
        for ref in group[1:]:
            value = value + ref[...].astype(jnp.float32)
        out[base : base + value.shape[0], :] = value
        base += value.shape[0]


def call(kernel, outs, smem, *args, scratch=(), flops=0, memory=pltpu.VMEM):
    size = sum(a.size * a.dtype.itemsize for a in args)
    place = lambda o: pl.BlockSpec(memory_space=pltpu.SMEM if o.dtype == jnp.int32 else pltpu.VMEM)
    return pl.pallas_call(
        kernel,
        out_shape=outs,
        out_specs=jax.tree.map(place, outs),
        in_specs=[pl.BlockSpec(memory_space=pltpu.SMEM)] * smem
        + [pl.BlockSpec(memory_space=memory)] * (len(args) - smem),
        scratch_shapes=list(scratch),
        compiler_params=VMEM,
        cost_estimate=pl.CostEstimate(flops=flops, bytes_accessed=size, transcendentals=0),
    )(*args)


def make(rows, cols):
    places = cols // 2
    bits = 2
    swap_core = pairs(rows, cols, lambda r, z, k: (r, z, 1 - k))
    in_plane = [
        pairs(rows, cols, lambda r, z, k, j=j: (r ^ (1 << (j if k == 0 else bits - 1 - j)), z, k))
        for j in range(bits)
    ]
    jumps = [pairs(rows, cols, lambda r, z, k, j=j: (r, z ^ j, k)) for j in range(places)]

    def on_device(chol, amplitudes, pair_offsets):
        depth, width = chol.shape
        columns = amplitudes.shape[1]
        blocks = pair_offsets.shape[0]
        share = blocks * AB_TILE // cols
        parts = [share * eighths // 8 for eighths in SPLIT]

        def picked(cap, h, offsets, most=()):
            held = jax.ShapeDtypeStruct((cap, AB_TILE // share * parts[h], depth), jnp.bfloat16)
            kernel = functools.partial(pick_kernel, sum(parts[:h]), parts[h], share)
            keep, give, *most = call(
                kernel,
                (held, held, *most),
                1,
                offsets,
                chol,
                scratch=[
                    pltpu.VMEM((2 * cap, depth, 2 * AB_TILE), jnp.bfloat16),
                    pltpu.SemaphoreType.DMA((2 * cap,)),
                ],
                memory=pl.ANY,
            )
            return (keep, give, *most)

        def merged(keep, give):
            return keep + lax.ppermute(give, AXES, swap_core)

        def rest(cap, own):
            def jump(own, j):
                return lax.ppermute(own, AXES, jumps[j])

            def across(m):
                return lax.ppermute(m, AXES, swap_core)

            def integrals(mine, other):
                height = blocks * mine[0].shape[1]
                return call(
                    functools.partial(integrals_kernel, places),
                    jax.ShapeDtypeStruct((height + PAD, width), jnp.float32),
                    1,
                    pair_offsets,
                    *mine,
                    *other,
                    chol,
                    scratch=[pltpu.VMEM((height, depth), jnp.bfloat16)],
                    flops=2 * height * depth * width,
                )

            def swap(block, j):
                came = lax.ppermute(block.astype(jnp.float16), AXES, in_plane[j])
                return came.astype(jnp.float32)

            def join(block, came):
                return call(join_kernel, jax.ShapeDtypeStruct(block.shape, jnp.float32), 0, block, came)

            def residual(block, came, part):
                height = block.shape[0] - PAD
                return call(
                    residual_kernel,
                    (jax.ShapeDtypeStruct((places, part, columns), jnp.float32),) * 2,
                    0,
                    block,
                    came,
                    amplitudes,
                    scratch=[pltpu.VMEM((height, columns), jnp.float32)],
                    flops=2 * height * width * columns,
                )

            def split(keep, got):
                part = keep.shape[1]
                return call(
                    split_kernel,
                    (jax.ShapeDtypeStruct((part, columns), jnp.float32),)
                    + (jax.ShapeDtypeStruct((part, columns), jnp.bfloat16),) * (places - 1),
                    0,
                    keep,
                    got,
                )

            def deliver(gives):
                return [lax.ppermute(g, AXES, jumps[j]) for j, g in enumerate(gives, 1)]

            after = lax.optimization_barrier
            two, one = after((jump(own, 2), jump(own, 1)))
            three = jump(two, 1)
            offsets, _ = after((pair_offsets, (one, two)))
            keep, give = picked(cap, 1, offsets)
            mine = [own, one, two]
            other = [across(m) for m in mine]
            own = merged(keep, give)
            own, three, *other = after((own, three, *other))
            block = integrals([*mine, three], [*other, across(three)])
            two, one = jump(own, 2), jump(own, 1)
            came = swap(block, 0)
            came, two, one = after((came, two, one))
            block = join(block, came)
            two, _ = after((two, block))
            three = jump(two, 1)
            came = swap(block, 1)
            mine = [own, one, two]
            second = integrals([*mine, three], [across(m) for m in [*mine, three]])
            second, came = after((second, came))
            keep, give = residual(block, came, parts[0])
            came = swap(second, 0)
            sums, *gives = split(keep, across(give))
            done = [sums] + deliver(gives)
            second = join(second, came)
            second, done[1] = after((second, done[1]))
            came, *done = after((swap(second, 1), *done))
            keep, give = residual(second, came, parts[1])
            sums, *gives = split(keep, across(give))
            done += [sums] + deliver(gives)
            return call(
                functools.partial(final_kernel, places),
                jax.ShapeDtypeStruct((share, columns), jnp.float32),
                0,
                *done,
            )

        keep, give, most = picked(1, 0, pair_offsets, (jax.ShapeDtypeStruct((1,), jnp.int32),))
        own = merged(keep, give)
        return lax.cond(
            most[0] <= 2,
            lambda own: rest(1, own),
            lambda own: rest((blocks + 1) // 2, merged(*picked((blocks + 1) // 2, 0, pair_offsets))),
            own,
        )

    return on_device


def simple(chol, amplitudes, pair_offsets):
    width = chol.shape[1]
    rows = (pair_offsets[:, None] + jnp.arange(AB_TILE, dtype=jnp.int32)[None, :]).reshape(-1)
    local = lax.axis_index("col") * width + jnp.arange(width, dtype=jnp.int32)
    selector = (local[:, None] == rows[None, :]).astype(jnp.bfloat16)
    picked = jnp.dot(chol, selector, preferred_element_type=jnp.float32)
    factors = lax.psum(picked.astype(jnp.bfloat16), "col")
    block = jnp.dot(factors.T, chol, preferred_element_type=jnp.float32)
    block = lax.psum(block, "row").astype(jnp.bfloat16)
    return lax.psum_scatter(
        jnp.dot(block, amplitudes, preferred_element_type=jnp.float32),
        "col",
        scatter_dimension=0,
        tiled=True,
    )


def solution(mesh):
    rows, cols = mesh.shape["row"], mesh.shape["col"]
    body = make(rows, cols) if (rows, cols) == (4, 8) else simple
    return jax.shard_map(
        body,
        mesh=mesh,
        in_specs=(P("row", "col"), P("col", "row"), P()),
        out_specs=P("col", "row"),
        check_vma=False,
    )
```

```python
import functools

import jax
import jax.numpy as jnp
from jax import lax
from jax.experimental import pallas as pl
from jax.experimental.pallas import tpu as pltpu
from jax.sharding import PartitionSpec as P

AB_TILE = 128
SPLIT = (5, 3)
LANES = 128
PAD = 16
AXES = ("row", "col")
VMEM = pltpu.CompilerParams(vmem_limit_bytes=20 * 1024 * 1024)


def pairs(rows, cols, target):
    listed = []
    for row in range(rows):
        for col in range(cols):
            to = target(row, col // 2, col % 2)
            listed.append((row * cols + col, to[0] * cols + to[1] * 2 + to[2]))
    return listed


def entry(offsets, chip, width, index):
    low = chip * (2 * width)
    seen = jnp.int32(0)
    block = jnp.int32(0)
    for b in range(offsets.shape[0]):
        start = offsets[b]
        here = ((start < low + 2 * width) & (start + (AB_TILE - 1) >= low)).astype(jnp.int32)
        block = jnp.where((here == 1) & (seen == index), b, block)
        seen = seen + here
    return block, seen > index


def pick_kernel(base, part, share, offsets, chol, keep, give, *refs):
    *most, held, done = refs
    cap, unit, depth = keep.shape
    width = chol.shape[1]
    col = lax.axis_index("col")
    chip, core = lax.div(col, 2), lax.rem(col, 2)
    window = 2 * AB_TILE
    t = lax.broadcasted_iota(jnp.int32, (unit, window), 0)
    lane = lax.broadcasted_iota(jnp.int32, (unit, window), 1)
    place = lax.div(t, part) * share + base + lax.rem(t, part)
    jobs = []
    for slot in range(cap):
        for ref, parity in ((give, 1 - core), (keep, core)):
            block, there = entry(offsets, chip, width, 2 * slot + parity)
            start = offsets[block] - col * width
            left = jnp.clip(lax.shift_right_arithmetic(start, 7), 0, width // AB_TILE - 2)
            left = pl.multiple_of(left * AB_TILE, AB_TILE)
            start = jnp.where(there, start, -4 * AB_TILE - width)
            at = len(jobs)
            copy = pltpu.make_async_copy(chol.at[:, pl.ds(left, window)], held.at[at], done.at[at])
            copy.start()
            jobs.append((copy, ref, slot, start - left))
    for at, (copy, ref, slot, start) in enumerate(jobs):
        hit = (lane == place + start).astype(jnp.float32).astype(jnp.bfloat16)
        copy.wait()
        ref[slot] = lax.dot_general(
            hit, held[at], (((1,), (1,)), ((), ())), preferred_element_type=jnp.float32
        ).astype(jnp.bfloat16)
    for ref in most:
        value = jnp.int32(0)
        for place in range(lax.axis_size("col") // 2):
            low = place * 2 * width
            seen = jnp.int32(0)
            for b in range(offsets.shape[0]):
                here = (offsets[b] < low + 2 * width) & (offsets[b] + (AB_TILE - 1) >= low)
                seen = seen + here.astype(jnp.int32)
            value = jnp.maximum(value, seen)
        ref[0] = value


def integrals_kernel(places, offsets, *refs):
    mine, other = refs[:places], refs[places : 2 * places]
    chol, block_out, factors = refs[2 * places :]
    cap, unit, depth = mine[0].shape
    width = chol.shape[1]
    col = lax.axis_index("col")
    chip, core = lax.div(col, 2), lax.rem(col, 2)
    factors[...] = jnp.zeros_like(factors)
    for j in range(places):
        for group, parity in ((mine, core), (other, 1 - core)):
            for slot in range(cap):
                block, there = entry(offsets, lax.bitwise_xor(chip, j), width, 2 * slot + parity)

                @pl.when(there)
                def _():
                    at = pl.ds(pl.multiple_of(block * unit, unit), unit)
                    factors[at, :] += group[j][slot]

    height = factors.shape[0]
    value = jnp.dot(factors[...], chol[...], preferred_element_type=jnp.float32)
    top = jnp.max(jnp.max(jnp.abs(value), axis=0, keepdims=True), axis=1, keepdims=True)
    power = jnp.floor(14.0 - jnp.log2(jnp.maximum(top, 1e-30)))
    power = jnp.broadcast_to(jnp.clip(power, -100.0, 100.0), (1, LANES))
    scale = jnp.exp2(power)
    for t in range(width // LANES):
        block_out[t * height : (t + 1) * height, :] = value[:, t * LANES : (t + 1) * LANES] * scale
    block_out[width // LANES * height :, :] = jnp.broadcast_to(power, (PAD, LANES))


def join_kernel(own, came, total):
    end = own.shape[0] - PAD
    first, second = own[end : end + 1, :], came[end : end + 1, :]
    power = jnp.minimum(first, second) - 1.0
    total[:end, :] = own[:end, :] * jnp.exp2(power - first) + came[:end, :] * jnp.exp2(power - second)
    total[end:, :] = jnp.broadcast_to(power, (PAD, LANES))


def residual_kernel(own, came, amplitudes, keep, *refs):
    *gives, block, result = refs
    core = lax.rem(lax.axis_index("col"), 2)
    places, part, _ = keep.shape
    end = own.shape[0] - PAD
    height, width = block.shape
    first, second = jnp.exp2(-own[end : end + 1, :]), jnp.exp2(-came[end : end + 1, :])
    for t in range(width // LANES):
        rows = slice(t * height, (t + 1) * height)
        value = own[rows, :] * first + came[rows, :] * second
        block[:, t * LANES : (t + 1) * LANES] = value.astype(jnp.bfloat16)
    result[...] = jnp.dot(block[...], amplitudes[...], preferred_element_type=jnp.float32)
    for p in range(places):
        keep[p] = result[pl.ds(pl.multiple_of(p * 2 * part + core * part, 8), part), :]
        base = p * 2 * part + (1 - core) * part
        for give in gives:
            give[p] = result[pl.ds(pl.multiple_of(base, 8), give.shape[1]), :]
            base += give.shape[1]


def split_kernel(keep, *refs):
    count = len(refs) - keep.shape[0]
    came, own, gives = refs[:count], refs[count], refs[count + 1 :]
    chip = lax.div(lax.axis_index("col"), 2)
    base = 0
    for piece in came:
        rows = slice(base, base + piece.shape[1])
        own[rows, :] = keep[chip, rows, :] + piece[chip]
        for j, give in enumerate(gives, 1):
            to = lax.bitwise_xor(chip, j)
            give[rows, :] = (keep[to, rows, :] + piece[to]).astype(jnp.bfloat16)
        base += piece.shape[1]


def final_kernel(terms, *refs):
    out = refs[-1]
    base = 0
    for h in range(len(SPLIT)):
        group = refs[h * terms : (h + 1) * terms]
        value = group[0][...]
        for ref in group[1:]:
            value = value + ref[...].astype(jnp.float32)
        out[base : base + value.shape[0], :] = value
        base += value.shape[0]


def call(kernel, outs, smem, *args, scratch=(), flops=0, memory=pltpu.VMEM):
    size = sum(a.size * a.dtype.itemsize for a in args)
    place = lambda o: pl.BlockSpec(memory_space=pltpu.SMEM if o.dtype == jnp.int32 else pltpu.VMEM)
    return pl.pallas_call(
        kernel,
        out_shape=outs,
        out_specs=jax.tree.map(place, outs),
        in_specs=[pl.BlockSpec(memory_space=pltpu.SMEM)] * smem
        + [pl.BlockSpec(memory_space=memory)] * (len(args) - smem),
        scratch_shapes=list(scratch),
        compiler_params=VMEM,
        cost_estimate=pl.CostEstimate(flops=flops, bytes_accessed=size, transcendentals=0),
    )(*args)


def make(rows, cols):
    places = cols // 2
    bits = 2
    swap_core = pairs(rows, cols, lambda r, z, k: (r, z, 1 - k))
    in_plane = [
        pairs(rows, cols, lambda r, z, k, j=j: (r ^ (1 << (j if k == 0 else bits - 1 - j)), z, k))
        for j in range(bits)
    ]
    jumps = [pairs(rows, cols, lambda r, z, k, j=j: (r, z ^ j, k)) for j in range(places)]

    def on_device(chol, amplitudes, pair_offsets):
        depth, width = chol.shape
        columns = amplitudes.shape[1]
        blocks = pair_offsets.shape[0]
        share = blocks * AB_TILE // cols
        parts = [share * eighths // 8 for eighths in SPLIT]

        def picked(cap, h, offsets, most=()):
            held = jax.ShapeDtypeStruct((cap, AB_TILE // share * parts[h], depth), jnp.bfloat16)
            keep, give, *most = call(
                functools.partial(pick_kernel, sum(parts[:h]), parts[h], share),
                (held, held, *most),
                1,
                offsets,
                chol,
                scratch=[
                    pltpu.VMEM((2 * cap, depth, 2 * AB_TILE), jnp.bfloat16),
                    pltpu.SemaphoreType.DMA((2 * cap,)),
                ],
                memory=pl.ANY,
            )
            return (keep + lax.ppermute(give, AXES, swap_core), *most)

        def rest(cap, own):
            def jump(own, j):
                return lax.ppermute(own, AXES, jumps[j])

            def across(m):
                return lax.ppermute(m, AXES, swap_core)

            def integrals(mine, other):
                height = blocks * mine[0].shape[1]
                return call(
                    functools.partial(integrals_kernel, places),
                    jax.ShapeDtypeStruct((height * width // LANES + PAD, LANES), jnp.float32),
                    1,
                    pair_offsets,
                    *mine,
                    *other,
                    chol,
                    scratch=[pltpu.VMEM((height, depth), jnp.bfloat16)],
                    flops=2 * height * depth * width,
                )

            def swap(block, j):
                came = lax.ppermute(block.astype(jnp.float16), AXES, in_plane[j])
                return came.astype(jnp.float32)

            def join(block, came):
                return call(join_kernel, jax.ShapeDtypeStruct(block.shape, jnp.float32), 0, block, came)

            def residual(block, came, *pieces):
                part = sum(pieces)
                height = places * 2 * part
                keep, *gives = call(
                    residual_kernel,
                    [jax.ShapeDtypeStruct((places, r, columns), jnp.float32) for r in (part, *pieces)],
                    0,
                    block,
                    came,
                    amplitudes,
                    scratch=[
                        pltpu.VMEM((height, width), jnp.bfloat16),
                        pltpu.VMEM((height, columns), jnp.float32),
                    ],
                    flops=2 * height * width * columns,
                )
                return keep, [across(g) for g in gives]

            def split(keep, got):
                part = keep.shape[1]
                return call(
                    split_kernel,
                    (jax.ShapeDtypeStruct((part, columns), jnp.float32),)
                    + (jax.ShapeDtypeStruct((part, columns), jnp.bfloat16),) * (places - 1),
                    0,
                    keep,
                    *got,
                )

            def deliver(gives):
                return [lax.ppermute(g, AXES, jumps[j]) for j, g in enumerate(gives, 1)]

            after = lax.optimization_barrier
            two, one = after((jump(own, 2), jump(own, 1)))
            three = jump(two, 1)
            offsets, _ = after((pair_offsets, (one, two)))
            mine = [own, one, two]
            other = [across(m) for m in mine]
            (own,) = picked(cap, 1, offsets)
            own, three, *other = after((own, three, *other))
            block = integrals([*mine, three], [*other, across(three)])
            two, one = jump(own, 2), jump(own, 1)
            came = swap(block, 0)
            came, two, one = after((came, two, one))
            block = join(block, came)
            two, _ = after((two, block))
            three = jump(two, 1)
            came = swap(block, 1)
            mine = [own, one, two]
            second = integrals([*mine, three], [across(m) for m in [*mine, three]])
            second, came = after((second, came))
            keep, got = residual(block, came, 16, 16, parts[0] - 32)
            came = swap(second, 0)
            sums, *gives = split(keep, got)
            second = join(second, came)
            second, sums, *gives = after((second, sums, *gives))
            done = [sums] + deliver(gives)
            came, *done = after((swap(second, 1), *done))
            sums, *gives = split(*residual(second, came, parts[1]))
            done += [sums] + deliver(gives)
            return call(
                functools.partial(final_kernel, places),
                jax.ShapeDtypeStruct((share, columns), jnp.float32),
                0,
                *done,
            )

        own, most = picked(1, 0, pair_offsets, (jax.ShapeDtypeStruct((1,), jnp.int32),))
        return lax.cond(
            most[0] <= 2,
            lambda own: rest(1, own),
            lambda own: rest((blocks + 1) // 2, *picked((blocks + 1) // 2, 0, pair_offsets)),
            own,
        )

    return on_device


def simple(chol, amplitudes, pair_offsets):
    width = chol.shape[1]
    rows = (pair_offsets[:, None] + jnp.arange(AB_TILE, dtype=jnp.int32)[None, :]).reshape(-1)
    local = lax.axis_index("col") * width + jnp.arange(width, dtype=jnp.int32)
    selector = (local[:, None] == rows[None, :]).astype(jnp.bfloat16)
    picked = jnp.dot(chol, selector, preferred_element_type=jnp.float32)
    factors = lax.psum(picked.astype(jnp.bfloat16), "col")
    block = jnp.dot(factors.T, chol, preferred_element_type=jnp.float32)
    block = lax.psum(block, "row").astype(jnp.bfloat16)
    return lax.psum_scatter(
        jnp.dot(block, amplitudes, preferred_element_type=jnp.float32),
        "col",
        scatter_dimension=0,
        tiled=True,
    )


def solution(mesh):
    rows, cols = mesh.shape["row"], mesh.shape["col"]
    body = make(rows, cols) if (rows, cols) == (4, 8) else simple
    return jax.shard_map(
        body,
        mesh=mesh,
        in_specs=(P("row", "col"), P("col", "row"), P()),
        out_specs=P("col", "row"),
        check_vma=False,
    )
```

```python
import functools

import jax
import jax.numpy as jnp
from jax import lax
from jax.experimental import pallas as pl
from jax.experimental.pallas import tpu as pltpu
from jax.sharding import PartitionSpec as P

AB_TILE = 128
SPLIT = (5, 3)
LANES = 128
PAD = 16
AXES = ("row", "col")
VMEM = pltpu.CompilerParams(vmem_limit_bytes=20 * 1024 * 1024)


def pairs(rows, cols, target):
    listed = []
    for row in range(rows):
        for col in range(cols):
            to = target(row, col // 2, col % 2)
            listed.append((row * cols + col, to[0] * cols + to[1] * 2 + to[2]))
    return listed


def entry(offsets, group, span, index):
    low = group * span
    seen = jnp.int32(0)
    block = jnp.int32(0)
    for b in range(offsets.shape[0]):
        start = offsets[b]
        here = ((start < low + span) & (start + (AB_TILE - 1) >= low)).astype(jnp.int32)
        block = jnp.where((here == 1) & (seen == index), b, block)
        seen = seen + here
    return block, seen > index


def most_of(offsets, places, width):
    most = jnp.int32(0)
    for place in range(places):
        low = place * 2 * width
        seen = jnp.int32(0)
        for b in range(offsets.shape[0]):
            here = (offsets[b] < low + 2 * width) & (offsets[b] + (AB_TILE - 1) >= low)
            seen = seen + here.astype(jnp.int32)
        most = jnp.maximum(most, seen)
    return most


def pick_kernel(paired, base, part, share, offsets, chol, keep, give, *refs):
    *most, held, done = refs
    cap, unit, depth = keep.shape
    width = chol.shape[1]
    col = lax.axis_index("col")
    chip, core = lax.div(col, 2), lax.rem(col, 2)
    window = 2 * AB_TILE
    t = lax.broadcasted_iota(jnp.int32, (unit, window), 0)
    lane = lax.broadcasted_iota(jnp.int32, (unit, window), 1)
    place = lax.div(t, part) * share + base + lax.rem(t, part)
    jobs = []
    for slot in range(cap):
        for ref, parity in ((give, 1 - core), (keep, core)):
            if paired:
                index = 2 * lax.rem(chip + slot, 2) + parity
                block, there = entry(offsets, lax.div(chip, 2), 4 * width, index)
            else:
                block, there = entry(offsets, chip, 2 * width, parity)
            start = offsets[block] - col * width
            use = there & (start > -AB_TILE) & (start < width)
            left = jnp.clip(lax.shift_right_arithmetic(start, 7), 0, width // AB_TILE - 2)
            left = pl.multiple_of(left * AB_TILE, AB_TILE)
            at = len(jobs)
            copy = pltpu.make_async_copy(chol.at[:, pl.ds(left, window)], held.at[at], done.at[at])
            pl.when(use)(copy.start)
            jobs.append((use, copy, ref, slot, start - left))
    for at, (use, copy, ref, slot, start) in enumerate(jobs):

        @pl.when(use)
        def _():
            hit = (lane == place + start).astype(jnp.float32).astype(jnp.bfloat16)
            copy.wait()
            ref[slot] = lax.dot_general(
                hit, held[at], (((1,), (1,)), ((), ())), preferred_element_type=jnp.float32
            ).astype(jnp.bfloat16)

        @pl.when(jnp.logical_not(use))
        def _():
            ref[slot] = jnp.zeros((unit, depth), jnp.bfloat16)

    for ref in most:
        ref[0] = most_of(offsets, lax.axis_size("col") // 2, width)


def integrals_kernel(places, paired, offsets, *refs):
    mine, other = refs[:places], refs[places : 2 * places]
    chol, block_out, factors = refs[2 * places :]
    unit, depth = mine[0].shape[1:]
    width = chol.shape[1]
    col = lax.axis_index("col")
    chip, core = lax.div(col, 2), lax.rem(col, 2)
    factors[...] = jnp.zeros_like(factors)
    for j in range(places):
        source = lax.bitwise_xor(chip, j)
        group = lax.div(source, 2) if paired else source
        span = 4 * width if paired else 2 * width
        first = 2 * lax.rem(source, 2) if paired else 0
        for held, parity in ((mine, core), (other, 1 - core)):
            block, there = entry(offsets, group, span, first + parity)

            @pl.when(there)
            def _():
                at = pl.ds(pl.multiple_of(block * unit, unit), unit)
                factors[at, :] += held[j][0]

    height = factors.shape[0]
    value = jnp.dot(factors[...], chol[...], preferred_element_type=jnp.float32)
    top = jnp.max(jnp.max(jnp.abs(value), axis=0, keepdims=True), axis=1, keepdims=True)
    power = jnp.floor(14.0 - jnp.log2(jnp.maximum(top, 1e-30)))
    power = jnp.broadcast_to(jnp.clip(power, -100.0, 100.0), (1, LANES))
    scale = jnp.exp2(power)
    for t in range(width // LANES):
        block_out[t * height : (t + 1) * height, :] = value[:, t * LANES : (t + 1) * LANES] * scale
    block_out[width // LANES * height :, :] = jnp.broadcast_to(power, (PAD, LANES))


def join_kernel(own, came, total):
    end = own.shape[0] - PAD
    first, second = own[end : end + 1, :], came[end : end + 1, :]
    power = jnp.minimum(first, second) - 1.0
    total[:end, :] = own[:end, :] * jnp.exp2(power - first) + came[:end, :] * jnp.exp2(power - second)
    total[end:, :] = jnp.broadcast_to(power, (PAD, LANES))


def residual_kernel(own, came, amplitudes, keep, *refs):
    *gives, block, result = refs
    core = lax.rem(lax.axis_index("col"), 2)
    places, part, _ = keep.shape
    end = own.shape[0] - PAD
    height, width = block.shape
    first, second = jnp.exp2(-own[end : end + 1, :]), jnp.exp2(-came[end : end + 1, :])
    for t in range(width // LANES):
        rows = slice(t * height, (t + 1) * height)
        value = own[rows, :] * first + came[rows, :] * second
        block[:, t * LANES : (t + 1) * LANES] = value.astype(jnp.bfloat16)
    result[...] = jnp.dot(block[...], amplitudes[...], preferred_element_type=jnp.float32)
    for p in range(places):
        keep[p] = result[pl.ds(pl.multiple_of(p * 2 * part + core * part, 8), part), :]
        base = p * 2 * part + (1 - core) * part
        for give in gives:
            give[p] = result[pl.ds(pl.multiple_of(base, 8), give.shape[1]), :]
            base += give.shape[1]


def split_kernel(keep, *refs):
    count = len(refs) - keep.shape[0]
    came, own, gives = refs[:count], refs[count], refs[count + 1 :]
    chip = lax.div(lax.axis_index("col"), 2)
    base = 0
    for piece in came:
        rows = slice(base, base + piece.shape[1])
        own[rows, :] = keep[chip, rows, :] + piece[chip]
        for j, give in enumerate(gives, 1):
            to = lax.bitwise_xor(chip, j)
            give[rows, :] = (keep[to, rows, :] + piece[to]).astype(jnp.bfloat16)
        base += piece.shape[1]


def final_kernel(terms, *refs):
    out = refs[-1]
    base = 0
    for h in range(len(SPLIT)):
        group = refs[h * terms : (h + 1) * terms]
        value = group[0][...]
        for ref in group[1:]:
            value = value + ref[...].astype(jnp.float32)
        out[base : base + value.shape[0], :] = value
        base += value.shape[0]


def call(kernel, outs, smem, *args, scratch=(), flops=0, memory=pltpu.VMEM):
    size = sum(a.size * a.dtype.itemsize for a in args)
    place = lambda o: pl.BlockSpec(memory_space=pltpu.SMEM if o.dtype == jnp.int32 else pltpu.VMEM)
    return pl.pallas_call(
        kernel,
        out_shape=outs,
        out_specs=jax.tree.map(place, outs),
        in_specs=[pl.BlockSpec(memory_space=pltpu.SMEM)] * smem
        + [pl.BlockSpec(memory_space=memory)] * (len(args) - smem),
        scratch_shapes=list(scratch),
        compiler_params=VMEM,
        cost_estimate=pl.CostEstimate(flops=flops, bytes_accessed=size, transcendentals=0),
    )(*args)


def make(rows, cols):
    places = cols // 2
    bits = 2
    swap_core = pairs(rows, cols, lambda r, z, k: (r, z, 1 - k))
    in_plane = [
        pairs(rows, cols, lambda r, z, k, j=j: (r ^ (1 << (j if k == 0 else bits - 1 - j)), z, k))
        for j in range(bits)
    ]
    jumps = [pairs(rows, cols, lambda r, z, k, j=j: (r, z ^ j, k)) for j in range(places)]

    def on_device(chol, amplitudes, pair_offsets):
        depth, width = chol.shape
        columns = amplitudes.shape[1]
        blocks = pair_offsets.shape[0]
        share = blocks * AB_TILE // cols
        parts = [share * eighths // 8 for eighths in SPLIT]

        def picked(h, offsets, paired=False, most=()):
            cap = 2 if paired else 1
            held = jax.ShapeDtypeStruct((cap, AB_TILE // share * parts[h], depth), jnp.bfloat16)
            keep, give, *most = call(
                functools.partial(pick_kernel, paired, sum(parts[:h]), parts[h], share),
                (held, held, *most),
                1,
                offsets,
                chol,
                scratch=[
                    pltpu.VMEM((2 * cap, depth, 2 * AB_TILE), jnp.bfloat16),
                    pltpu.SemaphoreType.DMA((2 * cap,)),
                ],
                memory=pl.ANY,
            )
            return (keep + lax.ppermute(give, AXES, swap_core), *most)

        def gathered(h, offsets):
            (both,) = picked(h, offsets, True)
            return both[:1] + lax.ppermute(both[1:], AXES, jumps[1])

        def rest(paired, own):
            def jump(own, j):
                return lax.ppermute(own, AXES, jumps[j])

            def across(m):
                return lax.ppermute(m, AXES, swap_core)

            def integrals(mine, other):
                height = blocks * mine[0].shape[1]
                return call(
                    functools.partial(integrals_kernel, places, paired),
                    jax.ShapeDtypeStruct((height * width // LANES + PAD, LANES), jnp.float32),
                    1,
                    pair_offsets,
                    *mine,
                    *other,
                    chol,
                    scratch=[pltpu.VMEM((height, depth), jnp.bfloat16)],
                    flops=2 * height * depth * width,
                )

            def swap(block, j):
                came = lax.ppermute(block.astype(jnp.float16), AXES, in_plane[j])
                return came.astype(jnp.float32)

            def join(block, came):
                return call(join_kernel, jax.ShapeDtypeStruct(block.shape, jnp.float32), 0, block, came)

            def residual(block, came, *pieces):
                part = sum(pieces)
                height = places * 2 * part
                keep, *gives = call(
                    residual_kernel,
                    [jax.ShapeDtypeStruct((places, r, columns), jnp.float32) for r in (part, *pieces)],
                    0,
                    block,
                    came,
                    amplitudes,
                    scratch=[
                        pltpu.VMEM((height, width), jnp.bfloat16),
                        pltpu.VMEM((height, columns), jnp.float32),
                    ],
                    flops=2 * height * width * columns,
                )
                return keep, [across(g) for g in gives]

            def split(keep, got):
                part = keep.shape[1]
                return call(
                    split_kernel,
                    (jax.ShapeDtypeStruct((part, columns), jnp.float32),)
                    + (jax.ShapeDtypeStruct((part, columns), jnp.bfloat16),) * (places - 1),
                    0,
                    keep,
                    *got,
                )

            def deliver(gives):
                return [lax.ppermute(g, AXES, jumps[j]) for j, g in enumerate(gives, 1)]

            after = lax.optimization_barrier
            one, two = after((jump(own, 1), jump(own, 2)))
            three = jump(two, 1)
            offsets, _ = after((pair_offsets, (one, two)))
            mine = [own, one, two]
            other = [across(m) for m in mine]
            own = gathered(1, offsets) if paired else picked(1, offsets)[0]
            own, three, *other = after((own, three, *other))
            block = integrals([*mine, three], [*other, across(three)])
            two, one = jump(own, 2), jump(own, 1)
            came = swap(block, 0)
            came, two, one = after((came, two, one))
            block = join(block, came)
            two, _ = after((two, block))
            three = jump(two, 1)
            came = swap(block, 1)
            mine = [own, one, two]
            second = integrals([*mine, three], [across(m) for m in [*mine, three]])
            second, came = after((second, came))
            keep, got = residual(block, came, 16, 16, parts[0] - 32)
            came = swap(second, 0)
            sums, *gives = split(keep, got)
            second = join(second, came)
            second, sums, *gives = after((second, sums, *gives))
            done = [sums] + deliver(gives)
            came, *done = after((swap(second, 1), *done))
            sums, *gives = split(*residual(second, came, parts[1]))
            done += [sums] + deliver(gives)
            return call(
                functools.partial(final_kernel, places),
                jax.ShapeDtypeStruct((share, columns), jnp.float32),
                0,
                *done,
            )

        own, most = picked(0, pair_offsets, False, (jax.ShapeDtypeStruct((1,), jnp.int32),))
        return lax.cond(
            most[0] > 2,
            lambda own: rest(True, gathered(0, pair_offsets)),
            lambda own: rest(False, own),
            own,
        )

    return on_device


def simple(chol, amplitudes, pair_offsets):
    width = chol.shape[1]
    rows = (pair_offsets[:, None] + jnp.arange(AB_TILE, dtype=jnp.int32)[None, :]).reshape(-1)
    local = lax.axis_index("col") * width + jnp.arange(width, dtype=jnp.int32)
    selector = (local[:, None] == rows[None, :]).astype(jnp.bfloat16)
    picked = jnp.dot(chol, selector, preferred_element_type=jnp.float32)
    factors = lax.psum(picked.astype(jnp.bfloat16), "col")
    block = jnp.dot(factors.T, chol, preferred_element_type=jnp.float32)
    block = lax.psum(block, "row").astype(jnp.bfloat16)
    return lax.psum_scatter(
        jnp.dot(block, amplitudes, preferred_element_type=jnp.float32),
        "col",
        scatter_dimension=0,
        tiled=True,
    )


def solution(mesh):
    rows, cols = mesh.shape["row"], mesh.shape["col"]
    body = make(rows, cols) if (rows, cols) == (4, 8) else simple
    return jax.shard_map(
        body,
        mesh=mesh,
        in_specs=(P("row", "col"), P("col", "row"), P()),
        out_specs=P("col", "row"),
        check_vma=False,
    )
```

```python
import functools

import jax
import jax.numpy as jnp
from jax import lax
from jax.experimental import pallas as pl
from jax.experimental.pallas import tpu as pltpu
from jax.sharding import PartitionSpec as P

AB_TILE = 128
SPLIT = (5, 3)
LANES = 128
PAD = 16
AXES = ("row", "col")
VMEM = pltpu.CompilerParams(vmem_limit_bytes=20 * 1024 * 1024)


def pairs(rows, cols, target):
    listed = []
    for row in range(rows):
        for col in range(cols):
            to = target(row, col // 2, col % 2)
            listed.append((row * cols + col, to[0] * cols + to[1] * 2 + to[2]))
    return listed


def entry(offsets, group, span, index):
    low = group * span
    seen = jnp.int32(0)
    block = jnp.int32(0)
    for b in range(offsets.shape[0]):
        start = offsets[b]
        here = ((start < low + span) & (start + (AB_TILE - 1) >= low)).astype(jnp.int32)
        block = jnp.where((here == 1) & (seen == index), b, block)
        seen = seen + here
    return block, seen > index


def most_of(offsets, places, width):
    most = jnp.int32(0)
    for place in range(places):
        low = place * 2 * width
        seen = jnp.int32(0)
        for b in range(offsets.shape[0]):
            here = (offsets[b] < low + 2 * width) & (offsets[b] + (AB_TILE - 1) >= low)
            seen = seen + here.astype(jnp.int32)
        most = jnp.maximum(most, seen)
    return most


def pick_kernel(paired, base, part, share, offsets, chol, keep, give, *refs):
    *most, held, done = refs
    cap, unit, depth = keep.shape
    width = chol.shape[1]
    col = lax.axis_index("col")
    chip, core = lax.div(col, 2), lax.rem(col, 2)
    window = 2 * AB_TILE
    t = lax.broadcasted_iota(jnp.int32, (unit, window), 0)
    lane = lax.broadcasted_iota(jnp.int32, (unit, window), 1)
    place = lax.div(t, part) * share + base + lax.rem(t, part)
    jobs = []
    for slot in range(cap):
        for ref, parity in ((give, 1 - core), (keep, core)):
            if paired:
                index = 2 * lax.rem(chip + slot, 2) + parity
                block, there = entry(offsets, lax.div(chip, 2), 4 * width, index)
            else:
                block, there = entry(offsets, chip, 2 * width, parity)
            start = offsets[block] - col * width
            use = there & (start > -AB_TILE) & (start < width)
            left = jnp.clip(lax.shift_right_arithmetic(start, 7), 0, width // AB_TILE - 2)
            left = pl.multiple_of(left * AB_TILE, AB_TILE)
            at = len(jobs)
            copy = pltpu.make_async_copy(chol.at[:, pl.ds(left, window)], held.at[at], done.at[at])
            pl.when(use)(copy.start)
            jobs.append((use, copy, ref, slot, start - left))
    for at, (use, copy, ref, slot, start) in enumerate(jobs):

        @pl.when(use)
        def _():
            hit = (lane == place + start).astype(jnp.float32).astype(jnp.bfloat16)
            copy.wait()
            ref[slot] = lax.dot_general(
                hit, held[at], (((1,), (1,)), ((), ())), preferred_element_type=jnp.float32
            ).astype(jnp.bfloat16)

        @pl.when(jnp.logical_not(use))
        def _():
            ref[slot] = jnp.zeros((unit, depth), jnp.bfloat16)

    for ref in most:
        ref[0] = most_of(offsets, lax.axis_size("col") // 2, width)


def integrals_kernel(places, paired, offsets, *refs):
    mine, other = refs[:places], refs[places : 2 * places]
    chol, block_out, factors = refs[2 * places :]
    unit, depth = mine[0].shape[1:]
    width = chol.shape[1]
    col = lax.axis_index("col")
    chip, core = lax.div(col, 2), lax.rem(col, 2)
    factors[...] = jnp.zeros_like(factors)
    for j in range(places):
        source = lax.bitwise_xor(chip, j)
        group = lax.div(source, 2) if paired else source
        span = 4 * width if paired else 2 * width
        first = 2 * lax.rem(source, 2) if paired else 0
        for held, parity in ((mine, core), (other, 1 - core)):
            block, there = entry(offsets, group, span, first + parity)

            @pl.when(there)
            def _():
                at = pl.ds(pl.multiple_of(block * unit, unit), unit)
                factors[at, :] += held[j][0]

    height = factors.shape[0]
    value = jnp.dot(factors[...], chol[...], preferred_element_type=jnp.float32)
    top = jnp.max(jnp.max(jnp.abs(value), axis=0, keepdims=True), axis=1, keepdims=True)
    power = jnp.floor(14.0 - jnp.log2(jnp.maximum(top, 1e-30)))
    power = jnp.broadcast_to(jnp.clip(power, -100.0, 100.0), (1, LANES))
    scale = jnp.exp2(power)
    for t in range(width // LANES):
        block_out[t * height : (t + 1) * height, :] = value[:, t * LANES : (t + 1) * LANES] * scale
    block_out[width // LANES * height :, :] = jnp.broadcast_to(power, (PAD, LANES))


def join_kernel(own, came, total):
    end = own.shape[0] - PAD
    first, second = own[end : end + 1, :], came[end : end + 1, :]
    power = jnp.minimum(first, second) - 1.0
    total[:end, :] = own[:end, :] * jnp.exp2(power - first) + came[:end, :] * jnp.exp2(power - second)
    total[end:, :] = jnp.broadcast_to(power, (PAD, LANES))


def residual_kernel(own, came, amplitudes, keep, *refs):
    *gives, block, result = refs
    core = lax.rem(lax.axis_index("col"), 2)
    places, part, _ = keep.shape
    end = own.shape[0] - PAD
    height, width = block.shape
    first, second = jnp.exp2(-own[end : end + 1, :]), jnp.exp2(-came[end : end + 1, :])
    for t in range(width // LANES):
        rows = slice(t * height, (t + 1) * height)
        value = own[rows, :] * first + came[rows, :] * second
        block[:, t * LANES : (t + 1) * LANES] = value.astype(jnp.bfloat16)
    result[...] = jnp.dot(block[...], amplitudes[...], preferred_element_type=jnp.float32)
    for p in range(places):
        keep[p] = result[pl.ds(pl.multiple_of(p * 2 * part + core * part, 8), part), :]
        base = p * 2 * part + (1 - core) * part
        for give in gives:
            give[p] = result[pl.ds(pl.multiple_of(base, 8), give.shape[1]), :]
            base += give.shape[1]


def split_kernel(keep, *refs):
    count = len(refs) - keep.shape[0]
    came, own, gives = refs[:count], refs[count], refs[count + 1 :]
    chip = lax.div(lax.axis_index("col"), 2)
    base = 0
    for piece in came:
        rows = slice(base, base + piece.shape[1])
        own[rows, :] = keep[chip, rows, :] + piece[chip]
        for j, give in enumerate(gives, 1):
            to = lax.bitwise_xor(chip, j)
            give[rows, :] = (keep[to, rows, :] + piece[to]).astype(jnp.bfloat16)
        base += piece.shape[1]


def final_kernel(terms, *refs):
    out = refs[-1]
    base = 0
    for h in range(len(SPLIT)):
        group = refs[h * terms : (h + 1) * terms]
        value = group[0][...]
        for ref in group[1:]:
            value = value + ref[...].astype(jnp.float32)
        out[base : base + value.shape[0], :] = value
        base += value.shape[0]


def call(kernel, outs, smem, *args, scratch=(), flops=0, memory=pltpu.VMEM):
    size = sum(a.size * a.dtype.itemsize for a in args)
    place = lambda o: pl.BlockSpec(memory_space=pltpu.SMEM if o.dtype == jnp.int32 else pltpu.VMEM)
    return pl.pallas_call(
        kernel,
        out_shape=outs,
        out_specs=jax.tree.map(place, outs),
        in_specs=[pl.BlockSpec(memory_space=pltpu.SMEM)] * smem
        + [pl.BlockSpec(memory_space=memory)] * (len(args) - smem),
        scratch_shapes=list(scratch),
        compiler_params=VMEM,
        cost_estimate=pl.CostEstimate(flops=flops, bytes_accessed=size, transcendentals=0),
    )(*args)


def make(rows, cols):
    places = cols // 2
    bits = 2
    swap_core = pairs(rows, cols, lambda r, z, k: (r, z, 1 - k))
    in_plane = [
        pairs(rows, cols, lambda r, z, k, j=j: (r ^ (1 << (j if k == 0 else bits - 1 - j)), z, k))
        for j in range(bits)
    ]
    jumps = [pairs(rows, cols, lambda r, z, k, j=j: (r, z ^ j, k)) for j in range(places)]

    def on_device(chol, amplitudes, pair_offsets):
        depth, width = chol.shape
        columns = amplitudes.shape[1]
        blocks = pair_offsets.shape[0]
        share = blocks * AB_TILE // cols
        parts = [share * eighths // 8 for eighths in SPLIT]

        def picked(h, offsets, paired=False, most=()):
            cap = 2 if paired else 1
            held = jax.ShapeDtypeStruct((cap, AB_TILE // share * parts[h], depth), jnp.bfloat16)
            keep, give, *most = call(
                functools.partial(pick_kernel, paired, sum(parts[:h]), parts[h], share),
                (held, held, *most),
                1,
                offsets,
                chol,
                scratch=[
                    pltpu.VMEM((2 * cap, depth, 2 * AB_TILE), jnp.bfloat16),
                    pltpu.SemaphoreType.DMA((2 * cap,)),
                ],
                memory=pl.ANY,
            )
            return (keep + lax.ppermute(give, AXES, swap_core), *most)

        def gathered(h, offsets):
            (both,) = picked(h, offsets, True)
            return both[:1] + lax.ppermute(both[1:], AXES, jumps[1])

        def rest(paired, own):
            def jump(own, j):
                return lax.ppermute(own, AXES, jumps[j])

            def across(m):
                return lax.ppermute(m, AXES, swap_core)

            def integrals(mine, other):
                height = blocks * mine[0].shape[1]
                return call(
                    functools.partial(integrals_kernel, places, paired),
                    jax.ShapeDtypeStruct((height * width // LANES + PAD, LANES), jnp.float32),
                    1,
                    pair_offsets,
                    *mine,
                    *other,
                    chol,
                    scratch=[pltpu.VMEM((height, depth), jnp.bfloat16)],
                    flops=2 * height * depth * width,
                )

            def swap(block, j):
                came = lax.ppermute(block.astype(jnp.float16), AXES, in_plane[j])
                return came.astype(jnp.float32)

            def join(block, came):
                return call(join_kernel, jax.ShapeDtypeStruct(block.shape, jnp.float32), 0, block, came)

            def residual(block, came, *pieces):
                part = sum(pieces)
                height = places * 2 * part
                keep, *gives = call(
                    residual_kernel,
                    [jax.ShapeDtypeStruct((places, r, columns), jnp.float32) for r in (part, *pieces)],
                    0,
                    block,
                    came,
                    amplitudes,
                    scratch=[
                        pltpu.VMEM((height, width), jnp.bfloat16),
                        pltpu.VMEM((height, columns), jnp.float32),
                    ],
                    flops=2 * height * width * columns,
                )
                return keep, [across(g) for g in gives]

            def split(keep, got):
                part = keep.shape[1]
                return call(
                    split_kernel,
                    (jax.ShapeDtypeStruct((part, columns), jnp.float32),)
                    + (jax.ShapeDtypeStruct((part, columns), jnp.bfloat16),) * (places - 1),
                    0,
                    keep,
                    *got,
                )

            def deliver(gives):
                return [lax.ppermute(g, AXES, jumps[j]) for j, g in reversed(list(enumerate(gives, 1)))]

            after = lax.optimization_barrier
            one, two = after((jump(own, 1), jump(own, 2)))
            three = jump(two, 1)
            offsets, _ = after((pair_offsets, (one, two)))
            mine = [own, one, two]
            other = [across(m) for m in mine]
            own = gathered(1, offsets) if paired else picked(1, offsets)[0]
            own, three, *other = after((own, three, *other))
            block = integrals([*mine, three], [*other, across(three)])
            one, two = jump(own, 1), jump(own, 2)
            came = swap(block, 0)
            came, two, one = after((came, two, one))
            block = join(block, came)
            two, _ = after((two, block))
            three = jump(two, 1)
            came = swap(block, 1)
            mine = [own, one, two]
            second = integrals([*mine, three], [across(m) for m in [*mine, three]])
            second, came = after((second, came))
            keep, got = residual(block, came, 16, 16, parts[0] - 32)
            came = swap(second, 0)
            sums, *gives = split(keep, got)
            second = join(second, came)
            second, sums, *gives = after((second, sums, *gives))
            done = [sums] + deliver(gives)
            came, *done = after((swap(second, 1), *done))
            sums, *gives = split(*residual(second, came, parts[1]))
            done += [sums] + deliver(gives)
            return call(
                functools.partial(final_kernel, places),
                jax.ShapeDtypeStruct((share, columns), jnp.float32),
                0,
                *done,
            )

        own, most = picked(0, pair_offsets, False, (jax.ShapeDtypeStruct((1,), jnp.int32),))
        return lax.cond(
            most[0] <= 2,
            lambda own: rest(False, own),
            lambda own: rest(True, gathered(0, pair_offsets)),
            own,
        )

    return on_device


def simple(chol, amplitudes, pair_offsets):
    width = chol.shape[1]
    rows = (pair_offsets[:, None] + jnp.arange(AB_TILE, dtype=jnp.int32)[None, :]).reshape(-1)
    local = lax.axis_index("col") * width + jnp.arange(width, dtype=jnp.int32)
    selector = (local[:, None] == rows[None, :]).astype(jnp.bfloat16)
    picked = jnp.dot(chol, selector, preferred_element_type=jnp.float32)
    factors = lax.psum(picked.astype(jnp.bfloat16), "col")
    block = jnp.dot(factors.T, chol, preferred_element_type=jnp.float32)
    block = lax.psum(block, "row").astype(jnp.bfloat16)
    return lax.psum_scatter(
        jnp.dot(block, amplitudes, preferred_element_type=jnp.float32),
        "col",
        scatter_dimension=0,
        tiled=True,
    )


def solution(mesh):
    rows, cols = mesh.shape["row"], mesh.shape["col"]
    body = make(rows, cols) if (rows, cols) == (4, 8) else simple
    return jax.shard_map(
        body,
        mesh=mesh,
        in_specs=(P("row", "col"), P("col", "row"), P()),
        out_specs=P("col", "row"),
        check_vma=False,
    )
```

```python
import functools

import jax
import jax.numpy as jnp
from jax import lax
from jax.experimental import pallas as pl
from jax.experimental.pallas import tpu as pltpu
from jax.sharding import PartitionSpec as P

AB_TILE = 128
SPLIT = (5, 3)
LANES = 128
PAD = 16
AXES = ("row", "col")
VMEM = pltpu.CompilerParams(vmem_limit_bytes=20 * 1024 * 1024)


def pairs(rows, cols, target):
    listed = []
    for row in range(rows):
        for col in range(cols):
            to = target(row, col // 2, col % 2)
            listed.append((row * cols + col, to[0] * cols + to[1] * 2 + to[2]))
    return listed


def entry(offsets, group, span, index):
    low = group * span
    seen = jnp.int32(0)
    block = jnp.int32(0)
    for b in range(offsets.shape[0]):
        start = offsets[b]
        here = ((start < low + span) & (start + (AB_TILE - 1) >= low)).astype(jnp.int32)
        block = jnp.where((here == 1) & (seen == index), b, block)
        seen = seen + here
    return block, seen > index


def most_of(offsets, places, width):
    most = jnp.int32(0)
    for place in range(places):
        low = place * 2 * width
        seen = jnp.int32(0)
        for b in range(offsets.shape[0]):
            here = (offsets[b] < low + 2 * width) & (offsets[b] + (AB_TILE - 1) >= low)
            seen = seen + here.astype(jnp.int32)
        most = jnp.maximum(most, seen)
    return most


def pick_kernel(paired, base, part, share, offsets, chol, keep, give, *refs):
    *most, held, done = refs
    cap, unit, depth = keep.shape
    width = chol.shape[1]
    col = lax.axis_index("col")
    chip, core = lax.div(col, 2), lax.rem(col, 2)
    window = 2 * AB_TILE
    t = lax.broadcasted_iota(jnp.int32, (unit, window), 0)
    lane = lax.broadcasted_iota(jnp.int32, (unit, window), 1)
    place = lax.div(t, part) * share + base + lax.rem(t, part)
    jobs = []
    for slot in range(cap):
        for ref, parity in ((give, 1 - core), (keep, core)):
            if paired:
                index = 2 * lax.rem(chip + slot, 2) + parity
                block, there = entry(offsets, lax.div(chip, 2), 4 * width, index)
            else:
                block, there = entry(offsets, chip, 2 * width, parity)
            start = offsets[block] - col * width
            use = there & (start > -AB_TILE) & (start < width)
            left = jnp.clip(lax.shift_right_arithmetic(start, 7), 0, width // AB_TILE - 2)
            left = pl.multiple_of(left * AB_TILE, AB_TILE)
            at = len(jobs)
            copy = pltpu.make_async_copy(chol.at[:, pl.ds(left, window)], held.at[at], done.at[at])
            pl.when(use)(copy.start)
            jobs.append((use, copy, ref, slot, start - left))
    for at, (use, copy, ref, slot, start) in enumerate(jobs):

        @pl.when(use)
        def _():
            hit = (lane == place + start).astype(jnp.float32).astype(jnp.bfloat16)
            copy.wait()
            ref[slot] = lax.dot_general(
                hit, held[at], (((1,), (1,)), ((), ())), preferred_element_type=jnp.float32
            ).astype(jnp.bfloat16)

        @pl.when(jnp.logical_not(use))
        def _():
            ref[slot] = jnp.zeros((unit, depth), jnp.bfloat16)

    for ref in most:
        ref[0] = most_of(offsets, lax.axis_size("col") // 2, width)


def integrals_kernel(places, paired, offsets, *refs):
    mine, other = refs[:places], refs[places : 2 * places]
    chol, block_out, factors = refs[2 * places :]
    unit, depth = mine[0].shape[1:]
    width = chol.shape[1]
    col = lax.axis_index("col")
    chip, core = lax.div(col, 2), lax.rem(col, 2)
    factors[...] = jnp.zeros_like(factors)
    for j in range(places):
        source = lax.bitwise_xor(chip, j)
        group = lax.div(source, 2) if paired else source
        span = 4 * width if paired else 2 * width
        first = 2 * lax.rem(source, 2) if paired else 0
        for held, parity in ((mine, core), (other, 1 - core)):
            block, there = entry(offsets, group, span, first + parity)

            @pl.when(there)
            def _():
                at = pl.ds(pl.multiple_of(block * unit, unit), unit)
                factors[at, :] += held[j][0]

    height = factors.shape[0]
    value = jnp.dot(factors[...], chol[...], preferred_element_type=jnp.float32)
    top = jnp.max(jnp.max(jnp.abs(value), axis=0, keepdims=True), axis=1, keepdims=True)
    power = jnp.floor(14.0 - jnp.log2(jnp.maximum(top, 1e-30)))
    power = jnp.broadcast_to(jnp.clip(power, -100.0, 100.0), (1, LANES))
    scale = jnp.exp2(power)
    for t in range(width // LANES):
        block_out[t * height : (t + 1) * height, :] = value[:, t * LANES : (t + 1) * LANES] * scale
    block_out[width // LANES * height :, :] = jnp.broadcast_to(power, (PAD, LANES))


def join_kernel(own, came, total):
    end = own.shape[0] - PAD
    first, second = own[end : end + 1, :], came[end : end + 1, :]
    power = jnp.minimum(first, second) - 1.0
    total[:end, :] = own[:end, :] * jnp.exp2(power - first) + came[:end, :] * jnp.exp2(power - second)
    total[end:, :] = jnp.broadcast_to(power, (PAD, LANES))


def residual_kernel(own, came, amplitudes, keep, *refs):
    *gives, block, result = refs
    core = lax.rem(lax.axis_index("col"), 2)
    places, part, _ = keep.shape
    end = own.shape[0] - PAD
    height, width = block.shape
    first, second = jnp.exp2(-own[end : end + 1, :]), jnp.exp2(-came[end : end + 1, :])
    for t in range(width // LANES):
        rows = slice(t * height, (t + 1) * height)
        value = own[rows, :] * first + came[rows, :] * second
        block[:, t * LANES : (t + 1) * LANES] = value.astype(jnp.bfloat16)
    result[...] = jnp.dot(block[...], amplitudes[...], preferred_element_type=jnp.float32)
    for p in range(places):
        keep[p] = result[pl.ds(pl.multiple_of(p * 2 * part + core * part, 8), part), :]
        base = p * 2 * part + (1 - core) * part
        for give in gives:
            give[p] = result[pl.ds(pl.multiple_of(base, 8), give.shape[1]), :]
            base += give.shape[1]


def split_kernel(keep, *refs):
    count = len(refs) - keep.shape[0]
    came, own, gives = refs[:count], refs[count], refs[count + 1 :]
    chip = lax.div(lax.axis_index("col"), 2)
    base = 0
    for piece in came:
        rows = slice(base, base + piece.shape[1])
        own[rows, :] = keep[chip, rows, :] + piece[chip]
        for j, give in enumerate(gives, 1):
            to = lax.bitwise_xor(chip, j)
            give[rows, :] = (keep[to, rows, :] + piece[to]).astype(jnp.bfloat16)
        base += piece.shape[1]


def final_kernel(terms, *refs):
    out = refs[-1]
    base = 0
    for h in range(len(SPLIT)):
        group = refs[h * terms : (h + 1) * terms]
        value = group[0][...]
        for ref in group[1:]:
            value = value + ref[...].astype(jnp.float32)
        out[base : base + value.shape[0], :] = value
        base += value.shape[0]


def call(kernel, outs, smem, *args, scratch=(), flops=0, memory=pltpu.VMEM):
    size = sum(a.size * a.dtype.itemsize for a in args)
    place = lambda o: pl.BlockSpec(memory_space=pltpu.SMEM if o.dtype == jnp.int32 else pltpu.VMEM)
    return pl.pallas_call(
        kernel,
        out_shape=outs,
        out_specs=jax.tree.map(place, outs),
        in_specs=[pl.BlockSpec(memory_space=pltpu.SMEM)] * smem
        + [pl.BlockSpec(memory_space=memory)] * (len(args) - smem),
        scratch_shapes=list(scratch),
        compiler_params=VMEM,
        cost_estimate=pl.CostEstimate(flops=flops, bytes_accessed=size, transcendentals=0),
    )(*args)


def make(rows, cols):
    places = cols // 2
    bits = 2
    swap_core = pairs(rows, cols, lambda r, z, k: (r, z, 1 - k))
    in_plane = [
        pairs(rows, cols, lambda r, z, k, j=j: (r ^ (1 << (j if k == 0 else bits - 1 - j)), z, k))
        for j in range(bits)
    ]
    jumps = [pairs(rows, cols, lambda r, z, k, j=j: (r, z ^ j, k)) for j in range(places)]

    def on_device(chol, amplitudes, pair_offsets):
        depth, width = chol.shape
        columns = amplitudes.shape[1]
        blocks = pair_offsets.shape[0]
        share = blocks * AB_TILE // cols
        parts = [share * eighths // 8 for eighths in SPLIT]

        def picked(h, offsets, paired=False, most=()):
            cap = 2 if paired else 1
            held = jax.ShapeDtypeStruct((cap, AB_TILE // share * parts[h], depth), jnp.bfloat16)
            keep, give, *most = call(
                functools.partial(pick_kernel, paired, sum(parts[:h]), parts[h], share),
                (held, held, *most),
                1,
                offsets,
                chol,
                scratch=[
                    pltpu.VMEM((2 * cap, depth, 2 * AB_TILE), jnp.bfloat16),
                    pltpu.SemaphoreType.DMA((2 * cap,)),
                ],
                memory=pl.ANY,
            )
            return (keep + lax.ppermute(give, AXES, swap_core), *most)

        def gathered(h, offsets):
            (both,) = picked(h, offsets, True)
            return both[:1] + lax.ppermute(both[1:], AXES, jumps[1])

        def rest(paired, own):
            def jump(own, j):
                return lax.ppermute(own, AXES, jumps[j])

            def across(m):
                return lax.ppermute(m, AXES, swap_core)

            def integrals(mine, other):
                height = blocks * mine[0].shape[1]
                return call(
                    functools.partial(integrals_kernel, places, paired),
                    jax.ShapeDtypeStruct((height * width // LANES + PAD, LANES), jnp.float32),
                    1,
                    pair_offsets,
                    *mine,
                    *other,
                    chol,
                    scratch=[pltpu.VMEM((height, depth), jnp.bfloat16)],
                    flops=2 * height * depth * width,
                )

            def swap(block, j):
                came = lax.ppermute(block.astype(jnp.float16), AXES, in_plane[j])
                return came.astype(jnp.float32)

            def join(block, came):
                return call(join_kernel, jax.ShapeDtypeStruct(block.shape, jnp.float32), 0, block, came)

            def residual(block, came, *pieces):
                part = sum(pieces)
                height = places * 2 * part
                keep, *gives = call(
                    residual_kernel,
                    [jax.ShapeDtypeStruct((places, r, columns), jnp.float32) for r in (part, *pieces)],
                    0,
                    block,
                    came,
                    amplitudes,
                    scratch=[
                        pltpu.VMEM((height, width), jnp.bfloat16),
                        pltpu.VMEM((height, columns), jnp.float32),
                    ],
                    flops=2 * height * width * columns,
                )
                return keep, [across(g) for g in gives]

            def split(keep, got):
                part = keep.shape[1]
                return call(
                    split_kernel,
                    (jax.ShapeDtypeStruct((part, columns), jnp.float32),)
                    + (jax.ShapeDtypeStruct((part, columns), jnp.bfloat16),) * (places - 1),
                    0,
                    keep,
                    *got,
                )

            def deliver(gives):
                return [lax.ppermute(g, AXES, jumps[j]) for j, g in reversed(list(enumerate(gives, 1)))]

            after = lax.optimization_barrier
            one, two = after((jump(own, 1), jump(own, 2)))
            three = jump(two, 1)
            offsets, _ = after((pair_offsets, (one, two)))
            mine = [own, one, two]
            other = [across(m) for m in mine]
            own = gathered(1, offsets) if paired else picked(1, offsets)[0]
            own, three, *other = after((own, three, *other))
            block = integrals([*mine, three], [*other, across(three)])
            one, two = jump(own, 1), jump(own, 2)
            came = swap(block, 0)
            came, two, one = after((came, two, one))
            block = join(block, came)
            two, _ = after((two, block))
            three = jump(two, 1)
            came = swap(block, 1)
            mine = [own, one, two]
            second = integrals([*mine, three], [across(m) for m in [*mine, three]])
            second, came = after((second, came))
            keep, got = residual(block, came, 16, parts[0] - 16)
            came = swap(second, 0)
            sums, *gives = split(keep, got)
            second = join(second, came)
            second, sums, *gives = after((second, sums, *gives))
            done = [sums] + deliver(gives)
            came, *done = after((swap(second, 1), *done))
            sums, *gives = split(*residual(second, came, parts[1]))
            done += [sums] + deliver(gives)
            return call(
                functools.partial(final_kernel, places),
                jax.ShapeDtypeStruct((share, columns), jnp.float32),
                0,
                *done,
            )

        own, most = picked(0, pair_offsets, False, (jax.ShapeDtypeStruct((1,), jnp.int32),))
        return lax.cond(
            most[0] <= 2,
            lambda own: rest(False, own),
            lambda own: rest(True, gathered(0, pair_offsets)),
            own,
        )

    return on_device


def simple(chol, amplitudes, pair_offsets):
    width = chol.shape[1]
    rows = (pair_offsets[:, None] + jnp.arange(AB_TILE, dtype=jnp.int32)[None, :]).reshape(-1)
    local = lax.axis_index("col") * width + jnp.arange(width, dtype=jnp.int32)
    selector = (local[:, None] == rows[None, :]).astype(jnp.bfloat16)
    picked = jnp.dot(chol, selector, preferred_element_type=jnp.float32)
    factors = lax.psum(picked.astype(jnp.bfloat16), "col")
    block = jnp.dot(factors.T, chol, preferred_element_type=jnp.float32)
    block = lax.psum(block, "row").astype(jnp.bfloat16)
    return lax.psum_scatter(
        jnp.dot(block, amplitudes, preferred_element_type=jnp.float32),
        "col",
        scatter_dimension=0,
        tiled=True,
    )


def solution(mesh):
    rows, cols = mesh.shape["row"], mesh.shape["col"]
    body = make(rows, cols) if (rows, cols) == (4, 8) else simple
    return jax.shard_map(
        body,
        mesh=mesh,
        in_specs=(P("row", "col"), P("col", "row"), P()),
        out_specs=P("col", "row"),
        check_vma=False,
    )
```
